32 devices in a mesh: dp: 8 (over y, x, core), tensor: 4 (over z).
Axes of the slice: x: 2, y: 2, z: 4, core: 2. Of those that a mesh axis runs over, the one named last changes fastest.
Arguments:
- tokens: bfloat16 [8192, 2560], P(('dp', 'tensor')), may hold values from -6 to 6
- cotangent: bfloat16 [8192, 2560], P(('dp', 'tensor')), may hold values from -6 to 6
- lengths: int32 [8, 3], P('dp'), may hold values from 1 to 576, 1024 in all within a row
- seq_deal: int32 [256], replicated, may hold values from 0 to 255, as said below
- mixer_gain: bfloat16 [2560], P('dp'), may hold values from 0.25 to 1.75
- recur_weight: bfloat16 [2560, 2560], P('dp', 'tensor'), may hold values from -0.125 to 0.125
- gelu_weight: bfloat16 [2560, 2560], P('dp', 'tensor'), may hold values from -0.125 to 0.125
- kernel_taps: bfloat16 [4, 2560], P(None, ('tensor', 'dp')), may hold values from -3 to 3
- kernel_bias: bfloat16 [2560], P(('tensor', 'dp')), may hold values from -3 to 3
- decay_param: bfloat16 [2560], P(('tensor', 'dp')), may hold values from 0.5 to 6
- rate_bias: bfloat16 [2560], P(('tensor', 'dp')), may hold values from -4 to 4
- input_bias: bfloat16 [2560], P(('tensor', 'dp')), may hold values from -4 to 4
- rate_blocks: bfloat16 [10, 256, 256], P(None, None, 'dp'), may hold values from -0.375 to 0.375
- input_blocks: bfloat16 [10, 256, 256], P(None, None, 'dp'), may hold values from -0.375 to 0.375
- mixer_out: bfloat16 [2560, 2560], P('tensor', 'dp'), may hold values from -0.3125 to 0.3125
- feed_gain: bfloat16 [2560], P('dp'), may hold values from 0.25 to 1.75
- feed_gate: bfloat16 [2560, 7680], P('dp', 'tensor'), may hold values from -0.125 to 0.125
- feed_up: bfloat16 [2560, 7680], P('dp', 'tensor'), may hold values from -0.125 to 0.125
- feed_down: bfloat16 [7680, 2560], P('tensor', 'dp'), may hold values from -0.09375 to 0.09375
Outputs:
- block_out: bfloat16 [8192, 2560], P(('dp', 'tensor'))
- tokens_grad: bfloat16 [8192, 2560], P(('dp', 'tensor'))
- grad_mixer_gain: float32 [2560], P('dp')
- grad_recur_weight: float32 [2560, 2560], P('dp', 'tensor')
- grad_gelu_weight: float32 [2560, 2560], P('dp', 'tensor')
- grad_kernel_taps: float32 [4, 2560], P(None, ('tensor', 'dp'))
- grad_kernel_bias: float32 [2560], P(('tensor', 'dp'))
- grad_decay_param: float32 [2560], P(('tensor', 'dp'))
- grad_rate_bias: float32 [2560], P(('tensor', 'dp'))
- grad_input_bias: float32 [2560], P(('tensor', 'dp'))
- grad_rate_blocks: float32 [10, 256, 256], P(None, None, 'dp')
- grad_input_blocks: float32 [10, 256, 256], P(None, None, 'dp')
- grad_mixer_out: float32 [2560, 2560], P('tensor', 'dp')
- grad_feed_gain: float32 [2560], P('dp')
- grad_feed_gate: float32 [2560, 7680], P('dp', 'tensor')
- grad_feed_up: float32 [2560, 7680], P('dp', 'tensor')
- grad_feed_down: float32 [7680, 2560], P('tensor', 'dp')
The draws below stay inside these ranges and needn't reach their ends.
Inputs may be any that keep to these rules, and one draw needn't show every extreme that they name: `seq_deal`: the pieces dealt to one device come one from each index of dp, from devices with the same index of tensor; the pieces that one device holds go to different indices of dp. `lengths`: each row sums to 1024 and its largest entry is 576.
All inputs are finite; a program needn't handle non-finite values.
Results may differ from the reference program's by a relative error of at most 0.02.
Values may be sent and summed in bfloat16 or wider, within the bound.
No kernel may reach another device: no remote copies, remote signals or barrier semaphores. Data moves between devices by JAX's collectives and lax.ppermute only.
A program may use at most 256 MiB of HBM per device.

```python
import math
import jax
import jax.numpy as jnp
import numpy as np
from jax import lax

D = 2560
HEADS = 10
BLOCK = 256
LRU = 2560
FF = 7680
TAPS = 4
SEQ_GRP = 3
TOK_GRP = 1024
MOST = 576
TOKENS = 8192
N_DP = 8
N_TENSOR = 4


def draw_seq_deal(key, part):
    device_total = N_DP * N_TENSOR
    send_keys = jax.random.split(jax.random.fold_in(key, 11), device_total)
    sender_target = jax.vmap(lambda one_key: jax.random.permutation(one_key, N_DP))(send_keys)
    recv_keys = jax.random.split(jax.random.fold_in(key, 23), device_total)
    source_groups = jax.vmap(lambda one_key: jax.random.permutation(one_key, N_DP))(recv_keys)
    slot_of_target = jnp.argsort(sender_target, axis=1).astype(jnp.int32)
    target_device = jnp.arange(device_total, dtype=jnp.int32)
    target_lane = target_device % N_TENSOR
    target_group = target_device // N_TENSOR
    source_device = (source_groups * N_TENSOR + target_lane[:, None]).astype(jnp.int32)
    source_slot = slot_of_target[source_device, jnp.broadcast_to(target_group[:, None], source_device.shape)]
    return (source_device * N_DP + source_slot).reshape(-1).astype(jnp.int32)


def block_levels(rng, extent, shards, low, largest):
    loudness = 1.0
    for position, blocks in shards:
        steps = jax.random.uniform(jax.random.fold_in(jax.random.fold_in(rng, 6), position), (blocks,), jnp.float32, low / len(shards), largest / len(shards))
        loudness = loudness * jnp.repeat(jnp.exp(steps), extent[position] // blocks).reshape((-1,) + (1,) * (len(extent) - 1 - position))
    return loudness


def split_up(number_of, total, bound, slope):
    portions = [(1 << 20) // math.isqrt(grade ** slope) + 1 for grade in range(2, number_of + 1)]
    surplus, holding = total - bound - (number_of - 1), [1] * (number_of - 1)
    while surplus > 0:
        candidates = [i for i in range(number_of - 1) if holding[i] < bound]
        pool, remaining = sum([portions[i] for i in candidates]), surplus
        for i in candidates:
            extra = min(bound - holding[i], max(1, remaining * portions[i] // pool), surplus)
            holding[i] = holding[i] + extra
            surplus = surplus - extra
    return np.array([bound] + holding)


def ragged(own_key, count, total, reach, lean):
    if count == 2:
        one = jax.random.randint(own_key, (), max(1, total - reach), min(reach, total - 1) + 1)
        return jnp.stack([one, total - one])
    sizes = jnp.asarray(split_up(count, total, reach, lean), jnp.int32)
    twos = (count - 1) // 2
    donor, sink = sizes[1:1 + 2 * twos:2], sizes[2:2 + 2 * twos:2]
    slack = jnp.minimum(donor - 1, reach - sink)
    moved = jax.random.randint(jax.random.fold_in(own_key, 1), (twos,), 0, 1 << 20) % (slack + 1)
    sizes = sizes.at[1:1 + 2 * twos:2].set(donor - moved).at[2:2 + 2 * twos:2].set(sink + moved)
    return sizes[jax.random.permutation(jax.random.fold_in(own_key, 2), count)]


def centred(own_key, extent, scale, bound, cuts=(), kind=jnp.bfloat16):
    level = block_levels(own_key, extent, cuts, -0.22, 0.18) if cuts else 1.0
    entries = jax.random.normal(own_key, extent, jnp.float32) * scale * level
    return jnp.minimum(jnp.maximum(entries, -bound), bound).astype(kind)


def setup_inputs(seed: int = 0) -> dict:
    streams_of = jax.random.split(jax.random.key(seed), 20)
    return {
        "tokens": centred(streams_of[0], (TOKENS, D), 1.0, 6.0, ((0, 32),)),
        "cotangent": centred(streams_of[1], (TOKENS, D), 1.0, 6.0, ((0, 32),)),
        "lengths": jax.vmap(lambda own: ragged(own, SEQ_GRP, TOK_GRP, MOST, 2))(jax.random.split(streams_of[2], N_DP)).reshape((N_DP, SEQ_GRP)).astype(jnp.int32),
        "seq_deal": draw_seq_deal(jax.random.fold_in(streams_of[19], 71), 0),
        "mixer_gain": jnp.clip(1.0 + 0.15 * jax.random.normal(streams_of[4], (D,), jnp.float32), 0.25, 1.75).astype(jnp.bfloat16),
        "recur_weight": centred(streams_of[5], (D, LRU), D ** -0.5, 0.125, ((0, 8), (1, 4))),
        "gelu_weight": centred(streams_of[6], (D, LRU), D ** -0.5, 0.125, ((0, 8), (1, 4))),
        "kernel_taps": centred(streams_of[7], (TAPS, LRU), 0.5, 3.0, ((1, 32),)),
        "kernel_bias": centred(streams_of[8], (LRU,), 0.5, 3.0, ((0, 32),)),
        "decay_param": jnp.clip(0.5 + 5.5 * jax.random.uniform(streams_of[9], (LRU,), jnp.float32) ** block_levels(streams_of[9], (LRU,), ((0, 32),), -0.2, 0.2), 0.5, 6.0).astype(jnp.bfloat16),
        "rate_bias": centred(streams_of[10], (LRU,), 1.0, 4.0, ((0, 32),)),
        "input_bias": centred(streams_of[11], (LRU,), 1.0, 4.0, ((0, 32),)),
        "rate_blocks": centred(streams_of[12], (HEADS, BLOCK, BLOCK), BLOCK ** -0.5, 0.375, ((2, 8),)),
        "input_blocks": centred(streams_of[13], (HEADS, BLOCK, BLOCK), BLOCK ** -0.5, 0.375, ((2, 8),)),
        "mixer_out": centred(streams_of[14], (LRU, D), (LRU // 8) ** -0.5, 0.3125, ((0, 4), (1, 8))),
        "feed_gain": jnp.clip(1.0 + 0.15 * jax.random.normal(streams_of[15], (D,), jnp.float32), 0.25, 1.75).astype(jnp.bfloat16),
        "feed_gate": centred(streams_of[16], (D, FF), D ** -0.5, 0.125, ((0, 8), (1, 4))),
        "feed_up": centred(streams_of[17], (D, FF), D ** -0.5, 0.125, ((0, 8), (1, 4))),
        "feed_down": centred(streams_of[18], (FF, D), (FF // 2) ** -0.5, 0.09375, ((0, 4), (1, 8))),
    }


@jax.custom_vjp
def low(v):
    return lax.optimization_barrier(v.astype(jnp.bfloat16)).astype(jnp.float32)

@jax.custom_vjp
def low_back(v):
    return v

def low_keep(v):
    return (low(v), None)

def low_pass(kept, grad):
    return (grad,)

def back_keep(v):
    return (v, None)

def back_low(kept, grad):
    return (low(grad),)
low.defvjp(low_keep, low_pass)
low_back.defvjp(back_keep, back_low)
norm_eps = 1e-06
scale_floor = 0.001

def product(left, right):
    return jnp.dot(left, right, precision=lax.Precision.HIGHEST, preferred_element_type=jnp.float32)

def smooth_gelu(values):
    return jax.nn.gelu(values, approximate=True)

def rms_norm(values, gain_vec):
    return values * lax.rsqrt(lax.optimization_barrier(jnp.mean(values * values, axis=-1, keepdims=True)) + norm_eps) * gain_vec

def positions(seq_lengths, row_total):
    ends = jnp.cumsum(seq_lengths).astype(jnp.int32)
    starts = ends - seq_lengths
    places = jnp.arange(row_total, dtype=jnp.int32)
    begins = lax.optimization_barrier(jnp.max(jnp.where(starts[None, :] <= places[:, None], starts[None, :], 0), axis=1))
    return places - begins

def causal_conv(values, taps, tap_bias, offset):
    tap_count = taps.shape[0]
    padded = jnp.pad(values, ((tap_count - 1, 0), (0, 0)))
    running = tap_bias[None, :] + jnp.zeros_like(values)
    for shift_lag in range(tap_count):
        shifted = padded[tap_count - 1 - shift_lag:tap_count - 1 - shift_lag + values.shape[0]]
        running = running + jnp.where((offset >= shift_lag)[:, None], shifted, 0.0) * taps[shift_lag][None, :]
    return running

def decay_input(pre_rate, pre_input, conv_out, decay_param, offset):
    rate_gate = jax.nn.sigmoid(pre_rate)
    input_gate = jax.nn.sigmoid(pre_input)
    log_decay = -8.0 * rate_gate * jax.nn.softplus(-decay_param)[None, :]
    decay_rate = jnp.where((offset == 0)[:, None], 0.0, jnp.exp(log_decay))
    input_scale = jnp.sqrt(jnp.maximum(1.0 - decay_rate * decay_rate, scale_floor))
    return (decay_rate, input_scale * input_gate * conv_out)

def combine(earlier, latter):
    return (earlier[0] * latter[0], latter[0] * earlier[1] + latter[1])

def block_diag(conv_out, blocks):
    row_total = conv_out.shape[0]
    head_view = conv_out.reshape(row_total, blocks.shape[0], blocks.shape[1])
    mixed_heads = jnp.einsum('thi,hij->thj', head_view, blocks, precision=lax.Precision.HIGHEST)
    return mixed_heads.reshape(row_total, -1)

def block(offset, x, mixer_gain, recur_weight, gelu_weight, kernel_taps, kernel_bias, decay_param, rate_bias, input_bias, rate_blocks, input_blocks, mixer_out, feed_gain, feed_gate, feed_up, feed_down):
    normed_first = low(rms_norm(x, mixer_gain))
    branch_y = low_back(product(normed_first, gelu_weight))
    branch_x = low_back(product(normed_first, recur_weight))
    conv_out = low(causal_conv(branch_x, kernel_taps, kernel_bias, offset))
    pre_rate = low_back(block_diag(conv_out, rate_blocks) + rate_bias)
    pre_input = low_back(block_diag(conv_out, input_blocks) + input_bias)
    decay_rate, driven = decay_input(pre_rate, pre_input, conv_out, decay_param, offset)
    _, lru_state = lax.associative_scan(combine, (decay_rate, driven))
    mixed_out = low(lru_state * smooth_gelu(branch_y))
    middle = x + low_back(product(mixed_out, mixer_out))
    normed_second = low(rms_norm(middle, feed_gain))
    gate_pre = low_back(product(normed_second, feed_gate))
    up_pre = low_back(product(normed_second, feed_up))
    hidden = low(smooth_gelu(gate_pre) * up_pre)
    return middle + low_back(product(hidden, feed_down))

def reference(tokens, cotangent, lengths, seq_deal, mixer_gain, recur_weight, gelu_weight, kernel_taps, kernel_bias, decay_param, rate_bias, input_bias, rate_blocks, input_blocks, mixer_out, feed_gain, feed_gate, feed_up, feed_down):
    piece_total = seq_deal.shape[0]
    piece_rows = tokens.shape[0] // piece_total

    def dealt(values_in):
        pieces = values_in.astype(jnp.float32).reshape(piece_total, piece_rows, -1)
        return jnp.take(pieces, seq_deal, axis=0).reshape(N_DP, TOK_GRP, -1)
    dealt_tokens = dealt(tokens)
    dealt_cot = dealt(cotangent)
    weights = tuple((weight.astype(jnp.float32) for weight in (mixer_gain, recur_weight, gelu_weight, kernel_taps, kernel_bias, decay_param, rate_bias, input_bias, rate_blocks, input_blocks, mixer_out, feed_gain, feed_gate, feed_up, feed_down)))
    zeros = tuple((jnp.zeros_like(weight) for weight in weights))

    def one_group(running, group_item):
        group_tokens, group_cot, seq_lengths = group_item
        offset = positions(seq_lengths, group_tokens.shape[0])

        def forward(x_in, *params):
            return block(offset, x_in, *params)
        output, pull_back = jax.vjp(forward, group_tokens, *weights)
        gradients = pull_back(group_cot)
        running = tuple((acc + grad_one for acc, grad_one in zip(running, gradients[1:])))
        return (running, (output.astype(jnp.bfloat16), gradients[0].astype(jnp.bfloat16)))
    sums, (outputs, input_grads) = lax.scan(one_group, zeros, (dealt_tokens, dealt_cot, lengths))

    def undeal(values_in):
        pieces = values_in.reshape(piece_total, piece_rows, -1)
        return jnp.zeros_like(pieces).at[seq_deal].set(pieces).reshape(tokens.shape[0], -1)
    return (undeal(outputs), undeal(input_grads), sums[0], sums[1], sums[2], sums[3], sums[4], sums[5], sums[6], sums[7], sums[8], sums[9], sums[10], sums[11], sums[12], sums[13], sums[14])
```

```python
import functools

import jax
import jax.numpy as jnp
from jax import lax
from jax.experimental import pallas as pl
from jax.experimental.pallas import tpu as pltpu
from jax.sharding import PartitionSpec as P

norm_eps = 1e-06
scale_floor = 0.001
halo = 8
bf16 = jnp.bfloat16
f32 = jnp.float32
gelu_c = 0.7978845608028654
gelu_k = 0.044715


def gelu_both(x):
    sq = x * x
    th = jnp.tanh(gelu_c * x * (1.0 + gelu_k * sq))
    half = 0.5 * (1.0 + th)
    return x * half, half + 0.5 * x * (1.0 - th * th) * gelu_c * (1.0 + 3.0 * gelu_k * sq)


def inv_rms(x):
    return lax.rsqrt(jnp.mean(x * x, axis=-1, keepdims=True) + norm_eps)


def norm_back(x, gain, grad):
    r = inv_rms(x)
    v = gain * grad
    dx = r * v - x * (r * r * r) * jnp.mean(x * v, axis=-1, keepdims=True)
    return dx, jnp.sum(grad * x * r, axis=0)


def mm(a, b):
    return jnp.dot(a, b, preferred_element_type=f32)


def mm_nt(a, b):
    return lax.dot_general(a, b, (((1,), (1,)), ((), ())), preferred_element_type=f32)


def mm_tn(a, b):
    return lax.dot_general(a, b, (((0,), (0,)), ((), ())), preferred_element_type=f32)


roomy = pltpu.CompilerParams(vmem_limit_bytes=56 * 1024 * 1024)


def cost(microseconds):
    return pl.CostEstimate(flops=int(microseconds * 1.15e9), bytes_accessed=1024, transcendentals=0)


def tile_of(total, most):
    for tile in range(most - most % 128, 0, -128):
        if total % tile == 0:
            return tile
    return total


def _pick_kernel(order_ref, x_ref, o_ref):
    for i in range(o_ref.shape[0]):
        o_ref[i] = x_ref[order_ref[i]]


def pick_pieces(pieces, order):
    return pl.pallas_call(
        _pick_kernel,
        in_specs=[pl.BlockSpec(memory_space=pltpu.SMEM), pl.BlockSpec(memory_space=pltpu.VMEM)],
        out_specs=pl.BlockSpec(memory_space=pltpu.VMEM),
        out_shape=jax.ShapeDtypeStruct(pieces.shape, pieces.dtype),
        name="pick_pieces", cost_estimate=cost(2),
    )(order, pieces)


def _turn_kernel(from_ref, x_ref, o_ref):
    width = x_ref.shape[1]
    place = lax.broadcasted_iota(jnp.int32, (width, o_ref.shape[1]), 0)
    hot = jnp.where(place == from_ref[...], 1.0, 0.0).astype(bf16)
    o_ref[...] = mm(x_ref[...], hot).astype(bf16)


def turn_feats(x, from_feat):
    rows, width = x.shape
    tile = tile_of(width, 512)
    return pl.pallas_call(
        _turn_kernel,
        grid=(width // tile,),
        in_specs=[pl.BlockSpec((1, tile), lambda j: (0, j)), pl.BlockSpec((rows, width), lambda j: (0, 0))],
        out_specs=pl.BlockSpec((rows, tile), lambda j: (0, j)),
        out_shape=jax.ShapeDtypeStruct(x.shape, bf16),
        compiler_params=roomy,
        name="turn_feats", cost_estimate=cost(6),
    )(from_feat[None], x)


def unit(n):
    one = lax.broadcasted_iota(jnp.int32, (n, n), 0) == lax.broadcasted_iota(jnp.int32, (n, n), 1)
    return jnp.where(one, 1.0, 0.0).astype(bf16)


def _flip_kernel(x_ref, o_ref):
    o_ref[...] = mm_tn(x_ref[...], unit(x_ref.shape[0])).astype(bf16)


def flip_weight(x):
    rows, cols = x.shape
    tile = tile_of(rows, 640)
    return pl.pallas_call(
        _flip_kernel,
        grid=(rows // tile,),
        in_specs=[pl.BlockSpec((tile, cols), lambda j: (j, 0))],
        out_specs=pl.BlockSpec((cols, tile), lambda j: (0, j)),
        out_shape=jax.ShapeDtypeStruct((cols, rows), bf16),
        compiler_params=roomy,
        name="flip_weight", cost_estimate=cost(4),
    )(x)


def _join_kernel(own_ref, x_ref, y_ref, low_ref, high_ref, out_ref):
    extra, feats = own_ref.shape[0], own_ref.shape[1]
    half = feats // 2
    for e in range(extra):
        for q, ref in enumerate((own_ref, x_ref, y_ref)):
            out_ref[(4 * e + q) * feats : (4 * e + q + 1) * feats] = ref[e]
        at = (4 * e + 3) * feats
        out_ref[at : at + half] = low_ref[e]
        out_ref[at + half : at + feats] = high_ref[e]


def join_feats(own, from_x, from_y, low, high):
    extra, feats, cols = own.shape
    tile = tile_of(cols, 640)
    full = pl.BlockSpec((extra, feats, tile), lambda j: (0, 0, j))
    part = pl.BlockSpec((extra, feats // 2, tile), lambda j: (0, 0, j))
    rows = extra * 4 * feats
    return pl.pallas_call(
        _join_kernel,
        grid=(cols // tile,),
        in_specs=[full, full, full, part, part],
        out_specs=pl.BlockSpec((rows, tile), lambda j: (0, j)),
        out_shape=jax.ShapeDtypeStruct((rows, cols), bf16),
        compiler_params=roomy,
        name="join_feats", cost_estimate=cost(5.5),
    )(own, from_x, from_y, low, high)


def _join_lanes_kernel(own_ref, x_ref, y_ref, low_ref, high_ref, out_ref):
    extra, feats = own_ref.shape[0], own_ref.shape[2]
    half = feats // 2
    for e in range(extra):
        for q, ref in enumerate((own_ref, x_ref, y_ref)):
            out_ref[0, (4 * e + q) * feats : (4 * e + q + 1) * feats] = ref[e, 0]
        at = (4 * e + 3) * feats
        out_ref[0, at : at + half] = low_ref[e, 0]
        out_ref[0, at + half : at + feats] = high_ref[e, 0]


def join_lanes(own, from_x, from_y, low, high):
    extra, lanes, feats, chans = own.shape
    full = pl.BlockSpec((extra, 1, feats, chans), lambda k: (0, k, 0, 0))
    part = pl.BlockSpec((extra, 1, feats // 2, chans), lambda k: (0, k, 0, 0))
    rows = extra * 4 * feats
    return pl.pallas_call(
        _join_lanes_kernel,
        grid=(lanes,),
        in_specs=[full, full, full, part, part],
        out_specs=pl.BlockSpec((1, rows, chans), lambda k: (k, 0, 0)),
        out_shape=jax.ShapeDtypeStruct((lanes, rows, chans), bf16),
        compiler_params=roomy,
        name="join_lanes",
        cost_estimate=cost(5),
    )(own, from_x, from_y, low, high)


def chan_spec(rows, chans):
    if chans % 128 == 0:
        return pl.BlockSpec((rows, chans), lambda k: (0, k))
    return pl.BlockSpec((1, rows, chans), lambda k: (k, 0, 0))


def chan_in(x, chans):
    if chans % 128 == 0:
        return x
    return jnp.swapaxes(x.reshape(x.shape[0], -1, chans), 0, 1)


def chan_get(ref):
    return ref[...] if len(ref.shape) == 2 else ref[0]


def rows_into(a, weight):
    rows, width = a.shape
    lanes, half, chans = weight[0].shape
    flat = chans % 128 == 0

    def kernel(a_ref, own_ref, other_ref, out_ref):
        got = mm(a_ref[:, :half], own_ref[0]) + mm(a_ref[:, half:], other_ref[0])
        if flat:
            out_ref[...] = got
        else:
            out_ref[0] = got

    block = pl.BlockSpec((1, half, chans), lambda k: (k, 0, 0))
    out = pl.pallas_call(
        kernel,
        grid=(lanes,),
        in_specs=[pl.BlockSpec((rows, width), lambda k: (0, 0)), block, block],
        out_specs=chan_spec(rows, chans),
        out_shape=jax.ShapeDtypeStruct((rows, lanes * chans) if flat else (lanes, rows, chans), f32),
        compiler_params=roomy,
        name="rows_into",
        cost_estimate=cost(11),
    )(a, *weight)
    return out if flat else jnp.swapaxes(out, 0, 1).reshape(rows, lanes * chans)


def rows_back(terms):
    rows = terms[0][0].shape[0]
    lanes, half, chans = terms[0][1][0].shape
    pairs = len(terms)

    def kernel(*refs):
        out_ref = refs[-1]

        @pl.when(pl.program_id(0) == 0)
        def _():
            out_ref[...] = jnp.zeros_like(out_ref)

        for side in range(2):
            total = None
            for p in range(pairs):
                part = mm_nt(chan_get(refs[p]), refs[pairs + 2 * p + side][0])
                total = part if total is None else total + part
            cols = slice(side * half, (side + 1) * half)
            out_ref[:, cols] = out_ref[:, cols] + total

    block = pl.BlockSpec((1, half, chans), lambda k: (k, 0, 0))
    arrays = [chan_in(b, chans) for b, _ in terms]
    for _, weight in terms:
        arrays += list(weight)
    return pl.pallas_call(
        kernel,
        grid=(lanes,),
        in_specs=[chan_spec(rows, chans)] * pairs + [block] * (2 * pairs),
        out_specs=pl.BlockSpec((rows, 2 * half), lambda k: (0, 0)),
        out_shape=jax.ShapeDtypeStruct((rows, 2 * half), f32),
        compiler_params=roomy,
        name="rows_back",
        cost_estimate=cost(8 * pairs + 3),
    )(*arrays)


def lane_block(lane, k, lanes):
    return lax.rem(lane[0] - k + lanes, lanes)


def feed_pair(ns, cot_all, at, gate, up, down, lane, lanes):
    count = len(ns)
    rows, width = ns[0].shape
    half, hidden = gate[0].shape
    tile = tile_of(hidden, 640)

    def kernel(lane_ref, *refs):
        ns_refs, cot_refs = refs[:count], refs[count : 2 * count]
        weights = refs[2 * count : 2 * count + 6]
        hid_ref, gate_ref, up_ref, ns_all, cot_rows = refs[2 * count + 6 :]

        @pl.when(pl.program_id(0) == 0)
        def _():
            for i in range(count):
                ns_all[i * rows : (i + 1) * rows] = ns_refs[i][...]
                cot_rows[i * rows : (i + 1) * rows] = cot_refs[i][...]

        def times(a, i):
            return mm(a[:, :half], weights[i][...]) + mm(a[:, half:], weights[i + 1][...])

        act, slope = gelu_both(times(ns_all, 0))
        up_pre = times(ns_all, 2)
        hid_ref[...] = (act * up_pre).astype(bf16)
        grad = times(cot_rows, 4)
        gate_ref[...] = (grad * up_pre * slope).astype(bf16)
        up_ref[...] = (grad * act).astype(bf16)

    whole = pl.BlockSpec((rows, width), lambda j, lane: (0, 0))
    cots = [
        pl.BlockSpec((rows, width), functools.partial(lambda j, lane, k: (lane_block(lane, k, lanes), 0), k=at + i))
        for i in range(count)
    ]
    piece = pl.BlockSpec((half, tile), lambda j, lane: (0, j))
    out = pl.BlockSpec((count * rows, tile), lambda j, lane: (0, j))
    return pl.pallas_call(
        kernel,
        grid_spec=pltpu.PrefetchScalarGridSpec(
            num_scalar_prefetch=1,
            grid=(hidden // tile,),
            in_specs=[whole] * count + cots + [piece] * 6,
            out_specs=[out] * 3,
            scratch_shapes=[pltpu.VMEM((count * rows, width), bf16)] * 2,
        ),
        out_shape=[jax.ShapeDtypeStruct((count * rows, hidden), bf16)] * 3,
        compiler_params=roomy,
        name="feed_pair",
        cost_estimate=cost(27),
    )(lane, *ns, *([cot_all] * count), *gate, *up, *down)


def feed_back(terms, at, rows, adds, kind):
    half, hidden = terms[0][1][0].shape
    width = 2 * half
    tile = tile_of(half, 640)
    steps = half // tile
    pairs = len(terms)

    def kernel(*refs):
        out_ref = refs[-1]
        j = pl.program_id(0)
        for side in range(2):

            @pl.when((j < steps) if side == 0 else (j >= steps))
            def _():
                total = None
                for p in range(pairs):
                    part = mm_nt(refs[p][...], refs[pairs + 2 * p + side][...])
                    total = part if total is None else total + part
                for extra_ref in refs[3 * pairs : -1]:
                    total = total + extra_ref[...].astype(f32)
                out_ref[...] = total.astype(kind)

    specs = [pl.BlockSpec((rows, hidden), lambda j: (at, 0))] * pairs
    arrays = [b for b, _ in terms]
    for _, weight in terms:
        specs.append(pl.BlockSpec((tile, hidden), lambda j: (jnp.minimum(j, steps - 1), 0)))
        specs.append(pl.BlockSpec((tile, hidden), lambda j: (jnp.maximum(j - steps, 0), 0)))
        arrays += list(weight)
    specs += [pl.BlockSpec((rows, tile), lambda j: (0, j))] * len(adds)
    return pl.pallas_call(
        kernel,
        grid=(2 * steps,),
        in_specs=specs,
        out_specs=pl.BlockSpec((rows, tile), lambda j: (0, j)),
        out_shape=jax.ShapeDtypeStruct((rows, width), kind),
        compiler_params=roomy,
        name="feed_back",
        cost_estimate=cost(13),
    )(*arrays, *adds)


def feed_out(hidden, weight, lane, lanes):
    half, units = weight[0].shape
    width = 2 * half
    tile = tile_of(half, 640)
    steps = half // tile
    many = len(hidden)
    count = lanes // many
    rows = hidden[0].shape[0] // count

    def kernel(lane_ref, *refs):
        out_ref = refs[-1]
        j = pl.program_id(0)
        for side in range(2):

            @pl.when((j < steps) if side == 0 else (j >= steps))
            def _():
                for i in range(many):
                    got = mm_nt(refs[i][...], refs[many + side][...]).astype(bf16)
                    for c in range(count):
                        at = lane_block(lane_ref, i * count + c, lanes) * rows
                        out_ref[pl.ds(pl.multiple_of(at, rows), rows)] = got[c * rows : (c + 1) * rows]

    whole = pl.BlockSpec((count * rows, units), lambda j, lane: (0, 0))
    return pl.pallas_call(
        kernel,
        grid_spec=pltpu.PrefetchScalarGridSpec(
            num_scalar_prefetch=1,
            grid=(2 * steps,),
            in_specs=[whole] * many
            + [
                pl.BlockSpec((tile, units), lambda j, lane: (jnp.minimum(j, steps - 1), 0)),
                pl.BlockSpec((tile, units), lambda j, lane: (jnp.maximum(j - steps, 0), 0)),
            ],
            out_specs=pl.BlockSpec((lanes * rows, tile), lambda j, lane: (0, j)),
        ),
        out_shape=jax.ShapeDtypeStruct((lanes * rows, width), bf16),
        compiler_params=roomy,
        name="feed_out",
        cost_estimate=cost(18),
    )(lane, *hidden, *weight)


def weight_grad(lefts, rights, side, feats, lane, lanes, got=None, by_lane=False):
    specs, arrays = [], []
    for left in lefts:
        if isinstance(left, tuple):
            array, left_rows, k = left
            pick = functools.partial(lambda j, lane, k: (lane_block(lane, k, lanes), side), k=k)
        else:
            array, left_rows, pick = left, left.shape[0], lambda j, lane: (0, side)
        half = array.shape[1] // 2
        specs.append(pl.BlockSpec((left_rows, half), pick))
        arrays.append(array)
    count = len(lefts)
    right_rows, cols = rights[0].shape
    many = len(rights)
    tile = cols // lanes if by_lane else tile_of(cols, 640)
    extra = half // (4 * feats)
    part = feats // 2

    def kernel(lane_ref, *refs):
        left_refs, right_refs = refs[:count], refs[count : count + many]
        rest = refs[count + many :]
        if count > 1:
            all_ref, rest = rest[-1], rest[:-1]

            @pl.when(pl.program_id(0) == 0)
            def _():
                for i in range(count):
                    all_ref[i * left_rows : (i + 1) * left_rows] = left_refs[i][...]
        else:
            all_ref = left_refs[0]
        total = None
        for i in range(many):
            piece = mm_tn(all_ref[i * right_rows : (i + 1) * right_rows], chan_get(right_refs[i]))
            total = piece if total is None else total + piece
        if got is None:
            if by_lane:
                rest[0][0] = total.astype(bf16)
            else:
                rest[0][...] = total.astype(bf16)
            return
        total = (total + chan_get(rest[0]).astype(f32)).astype(bf16)
        cuts = (0, feats, 2 * feats, 3 * feats, 3 * feats + part, 4 * feats)
        for e in range(extra):
            base = 4 * feats * e
            for ref, a, b in zip(rest[1:], cuts[:-1], cuts[1:]):
                if by_lane:
                    ref[e, 0] = total[base + a : base + b]
                else:
                    ref[e] = total[base + a : base + b]

    flat = not by_lane or tile % 128 == 0
    if flat:
        right_spec = pl.BlockSpec((right_rows, tile), lambda j, lane: (0, j))
    else:
        right_spec = pl.BlockSpec((1, right_rows, tile), lambda j, lane: (j, 0, 0))
        rights = [chan_in(r, tile) for r in rights]
    if by_lane:
        sent, sent_shape = pl.BlockSpec((1, half, tile), lambda j, lane: (j, 0, 0)), (lanes, half, tile)
        block = lambda n: pl.BlockSpec((extra, 1, n, tile), lambda j, lane: (0, j, 0, 0))
        block_shape = lambda n: (extra, lanes, n, tile)
    else:
        sent, sent_shape = pl.BlockSpec((half, tile), lambda j, lane: (0, j)), (half, cols)
        block = lambda n: pl.BlockSpec((extra, n, tile), lambda j, lane: (0, 0, j))
        block_shape = lambda n: (extra, n, cols)
    sizes = (feats, feats, feats, part, part)
    specs += [right_spec] * many
    arrays += list(rights)
    if got is None:
        out_specs, out_shape = sent, jax.ShapeDtypeStruct(sent_shape, bf16)
    else:
        specs.append(sent)
        arrays.append(got)
        out_specs = [block(n) for n in sizes]
        out_shape = [jax.ShapeDtypeStruct(block_shape(n), bf16) for n in sizes]
    return pl.pallas_call(
        kernel,
        grid_spec=pltpu.PrefetchScalarGridSpec(
            num_scalar_prefetch=1,
            grid=(cols // tile,),
            in_specs=specs,
            out_specs=out_specs,
            scratch_shapes=[pltpu.VMEM((left_rows * count, half), bf16)] if count > 1 else [],
        ),
        out_shape=out_shape,
        compiler_params=roomy,
        name="weight_grad",
        cost_estimate=cost(10 if count > 1 else 7),
    )(lane, *arrays)


def scan_rows(a, b, reverse):
    rows = a.shape[0]
    place = lax.broadcasted_iota(jnp.int32, a.shape, 0)
    step = 1
    while step < rows:
        if reverse:
            inside = place < rows - step
            turn = rows - step
        else:
            inside = place >= step
            turn = step
        a_far = jnp.where(inside, pltpu.roll(a, turn, 0), 1.0)
        b_far = jnp.where(inside, pltpu.roll(b, turn, 0), 0.0)
        b = a * b_far + b
        a = a * a_far
        step *= 2
    return a, b


def gate_values(conv_low, rate_t, input_t, vec, first):
    q = jax.nn.sigmoid(mm_nt(conv_low, rate_t) + vec[5:6])
    p = jax.nn.sigmoid(mm_nt(conv_low, input_t) + vec[6:7])
    decay = jnp.where(first, 0.0, jnp.exp(-8.0 * q * vec[7:8]))
    room = 1.0 - decay * decay
    scale = jnp.sqrt(jnp.maximum(room, scale_floor))
    return q, p, decay, room, scale


def _mix_fwd_kernel(bx_ref, off_ref, vec_ref, rate_ref, input_ref, conv_ref, state_ref, prod_ref):
    rows = conv_ref.shape[0]
    off = off_ref[0:rows]
    vec = vec_ref[...]
    conv = jnp.broadcast_to(vec[4:5], state_ref.shape)
    for lag in range(4):
        conv = conv + jnp.where(off >= lag, bx_ref[halo - lag : halo - lag + rows], 0.0) * vec[lag : lag + 1]
    conv_low = conv.astype(bf16)
    conv_ref[...] = conv_low
    q, p, decay, room, scale = gate_values(conv_low, rate_ref[0], input_ref[0], vec, off == 0)
    driven = scale * p * conv_low.astype(f32)
    prod, state = scan_rows(decay, driven, False)
    state_ref[...] = state
    prod_ref[...] = prod


def mix_fwd(bx_ext, off_ext, vec, rate_t, input_t):
    heads, width, _ = rate_t.shape
    ext = bx_ext.shape[0]
    rows = ext - halo
    col = lambda h: (0, h)
    return pl.pallas_call(
        _mix_fwd_kernel,
        grid=(heads,),
        in_specs=[
            pl.BlockSpec((ext, width), col),
            pl.BlockSpec((ext, 1), lambda h: (0, 0)),
            pl.BlockSpec((16, width), col),
            pl.BlockSpec((1, width, width), lambda h: (h, 0, 0)),
            pl.BlockSpec((1, width, width), lambda h: (h, 0, 0)),
        ],
        out_specs=[pl.BlockSpec((rows, width), col)] * 3,
        out_shape=[
            jax.ShapeDtypeStruct((rows, heads * width), bf16),
            jax.ShapeDtypeStruct((rows, heads * width), f32),
            jax.ShapeDtypeStruct((rows, heads * width), f32),
        ],
        name="mix_fwd", cost_estimate=cost(12),
    )(bx_ext, off_ext, vec, rate_t, input_t)


def _mix_out_kernel(state_ref, prod_ref, enter_ref, by_ref, full_ref, mixed_ref):
    state = state_ref[...] + prod_ref[...] * enter_ref[0:1]
    full_ref[...] = state
    act, _ = gelu_both(by_ref[...])
    mixed_ref[...] = (state * act).astype(bf16)


def mix_out(state, prod, enter, by, width):
    rows, total = state.shape
    blk = pl.BlockSpec((rows, width), lambda h: (0, h))
    return pl.pallas_call(
        _mix_out_kernel,
        grid=(total // width,),
        in_specs=[blk, blk, pl.BlockSpec((8, width), lambda h: (0, h)), blk],
        out_specs=[blk, blk],
        out_shape=[jax.ShapeDtypeStruct((rows, total), f32), jax.ShapeDtypeStruct((rows, total), bf16)],
        name="mix_out", cost_estimate=cost(6),
    )(state, prod, enter, by)


def _mix_adj_kernel(gm_ref, by_ref, full_ref, conv_ref, off_ref, vec_ref, rate_ref, gy_ref, adj_ref, tail_ref, edge_ref):
    rows = conv_ref.shape[0]
    vec = vec_ref[...]
    off = off_ref[0:rows]
    q = jax.nn.sigmoid(mm_nt(conv_ref[...], rate_ref[0]) + vec[5:6])
    decay = jnp.where(off == 0, 0.0, jnp.exp(-8.0 * q * vec[7:8]))
    act, act_grad = gelu_both(by_ref[...])
    gm = gm_ref[...]
    gy_ref[...] = (gm * full_ref[...] * act_grad).astype(bf16)
    place = lax.broadcasted_iota(jnp.int32, decay.shape, 0)
    after = jnp.where(place == rows - 1, 1.0, pltpu.roll(decay, rows - 1, 0))
    tail, adj = scan_rows(after, gm * act, True)
    adj_ref[...] = adj
    tail_ref[...] = tail
    edge_ref[0:1] = decay[0:1] * adj[0:1]
    edge_ref[1:2] = decay[0:1] * tail[0:1]
    edge_ref[2:8] = jnp.zeros((6, decay.shape[1]), f32)


def mix_adj(gm, by, full, conv, off_ext, vec, rate_t):
    heads, width, _ = rate_t.shape
    rows, total = gm.shape
    blk = pl.BlockSpec((rows, width), lambda h: (0, h))
    return pl.pallas_call(
        _mix_adj_kernel,
        grid=(heads,),
        in_specs=[
            blk,
            blk,
            blk,
            blk,
            pl.BlockSpec((rows + halo, 1), lambda h: (0, 0)),
            pl.BlockSpec((16, width), lambda h: (0, h)),
            pl.BlockSpec((1, width, width), lambda h: (h, 0, 0)),
        ],
        out_specs=[blk, blk, blk, pl.BlockSpec((8, width), lambda h: (0, h))],
        out_shape=[
            jax.ShapeDtypeStruct((rows, total), bf16),
            jax.ShapeDtypeStruct((rows, total), f32),
            jax.ShapeDtypeStruct((rows, total), f32),
            jax.ShapeDtypeStruct((8, total), f32),
        ],
        name="mix_adj", cost_estimate=cost(13),
    )(gm, by, full, conv, off_ext, vec, rate_t)


def _mix_bwd_kernel(
    adj_ref, tail_ref, hand_ref, full_ref, enter_ref, conv_ref, off_ref, vec_ref, rate_ref, input_ref,
    gc_ref, drate_ref, dinput_ref, sums_ref,
):
    rows = conv_ref.shape[0]
    vec = vec_ref[...]
    off = off_ref[0:rows]
    conv_low = conv_ref[...]
    conv = conv_low.astype(f32)
    rate_t, input_t = rate_ref[0], input_ref[0]
    q, p, decay, room, scale = gate_values(conv_low, rate_t, input_t, vec, off == 0)
    adj = adj_ref[...] + tail_ref[...] * hand_ref[0:1]
    place = lax.broadcasted_iota(jnp.int32, adj.shape, 0)
    before = jnp.where(place == 0, enter_ref[0:1], pltpu.roll(full_ref[...], 1, 0))
    g_decay = adj * before - jnp.where(room > scale_floor, adj * p * conv * decay / scale, 0.0)
    g_log = g_decay * decay
    g_rate = (-8.0 * g_log * vec[7:8] * q * (1.0 - q)).astype(bf16)
    g_input = (adj * scale * conv * p * (1.0 - p)).astype(bf16)
    gc_ref[...] = adj * scale * p + mm(g_rate, rate_t) + mm(g_input, input_t)
    drate_ref[0] = mm_tn(g_rate, conv_low).astype(bf16)
    dinput_ref[0] = mm_tn(g_input, conv_low).astype(bf16)
    sums_ref[0:1] = jnp.sum(8.0 * g_log * q, axis=0, keepdims=True) * vec[8:9]
    sums_ref[1:2] = jnp.sum(g_rate.astype(f32), axis=0, keepdims=True)
    sums_ref[2:3] = jnp.sum(g_input.astype(f32), axis=0, keepdims=True)
    sums_ref[3:8] = jnp.zeros((5, adj.shape[1]), f32)


def mix_bwd(adj, tail, hand, full, enter, conv, off_ext, vec, rate_t, input_t):
    heads, width, _ = rate_t.shape
    rows, total = adj.shape
    col = lambda h: (0, h)
    blk = pl.BlockSpec((rows, width), col)
    row8 = pl.BlockSpec((8, width), col)
    square = pl.BlockSpec((1, width, width), lambda h: (h, 0, 0))
    return pl.pallas_call(
        _mix_bwd_kernel,
        grid=(heads,),
        in_specs=[
            blk, blk, row8, blk, row8, blk,
            pl.BlockSpec((rows + halo, 1), lambda h: (0, 0)),
            pl.BlockSpec((16, width), col),
            square, square,
        ],
        out_specs=[blk, square, square, row8],
        out_shape=[
            jax.ShapeDtypeStruct((rows, total), f32),
            jax.ShapeDtypeStruct((heads, width, width), bf16),
            jax.ShapeDtypeStruct((heads, width, width), bf16),
            jax.ShapeDtypeStruct((8, total), f32),
        ],
        name="mix_bwd", cost_estimate=cost(14),
    )(adj, tail, hand, full, enter, conv, off_ext, vec, rate_t, input_t)


def _conv_bwd_kernel(gc_ref, next_ref, bx_ref, off_ref, vec_ref, gx_ref, sums_ref, ext_ref):
    rows = gc_ref.shape[0]
    vec = vec_ref[...]
    gc = gc_ref[...]
    ext_ref[0:rows] = gc
    ext_ref[rows : rows + halo] = next_ref[...]
    off = off_ref[0:rows]
    gx = gc * vec[0:1]
    sums_ref[0:1] = jnp.sum(gc * bx_ref[halo : halo + rows], axis=0, keepdims=True)
    for lag in range(1, 4):
        gx = gx + jnp.where(off_ref[lag : lag + rows] >= lag, ext_ref[lag : lag + rows], 0.0) * vec[lag : lag + 1]
        term = jnp.where(off >= lag, gc * bx_ref[halo - lag : halo - lag + rows], 0.0)
        sums_ref[lag : lag + 1] = jnp.sum(term, axis=0, keepdims=True)
    sums_ref[4:5] = jnp.sum(gc, axis=0, keepdims=True)
    sums_ref[5:8] = jnp.zeros((3, gc.shape[1]), f32)
    gx_ref[...] = gx.astype(bf16)


def conv_bwd(gc, gc_next, bx_ext, off_ext, vec, width):
    rows, total = gc.shape
    col = lambda h: (0, h)
    return pl.pallas_call(
        _conv_bwd_kernel,
        grid=(total // width,),
        in_specs=[
            pl.BlockSpec((rows, width), col),
            pl.BlockSpec((halo, width), col),
            pl.BlockSpec((rows + halo, width), col),
            pl.BlockSpec((rows + halo, 1), lambda h: (0, 0)),
            pl.BlockSpec((16, width), col),
        ],
        out_specs=[pl.BlockSpec((rows, width), col), pl.BlockSpec((8, width), col)],
        out_shape=[jax.ShapeDtypeStruct((rows, total), bf16), jax.ShapeDtypeStruct((8, total), f32)],
        scratch_shapes=[pltpu.VMEM((rows + halo, width), f32)],
        name="conv_bwd", cost_estimate=cost(7),
    )(gc, gc_next, bx_ext, off_ext, vec)


def after(x, *deps):
    return lax.optimization_barrier((x, deps))[0]


def per_device(
    tokens, cotangent, lengths, seq_deal, mixer_gain, recur_weight, gelu_weight, kernel_taps, kernel_bias,
    decay_param, rate_bias, input_bias, rate_blocks, input_blocks, mixer_out, feed_gain, feed_gate, feed_up,
    feed_down,
):
    groups = lax.axis_size("dp")
    lanes = lax.axis_size("tensor")
    bits = groups.bit_length() - 1
    g = lax.axis_index("dp")
    t = lax.axis_index("tensor")
    lane = t[None].astype(jnp.int32)
    device = g * lanes + t
    rows, width = tokens.shape
    piece_rows = rows // groups
    feats = mixer_gain.shape[0]
    chans = recur_weight.shape[1]
    lru_total = chans * lanes
    head_width = rate_blocks.shape[1]
    wide = tile_of(lru_total, 640)

    def swap(x, bit):
        return lax.ppermute(x, "dp", [(i, i ^ (1 << bit)) for i in range(groups)])

    def up(x):
        return lax.ppermute(x, "tensor", [(i, (i + 1) % lanes) for i in range(lanes)])

    def shift(x, by):
        return lax.ppermute(x, "tensor", [(i, i + by) for i in range(lanes) if 0 <= i + by < lanes])

    def gather_outer(part, *deps):
        part = (after(part, *deps) if deps else part)[None]
        for bit in range(3, bits):
            part = jnp.concatenate([part, swap(part, bit)], axis=0)
        from_x, from_y = swap(part, 1), swap(part, 2)
        half = feats // 2
        low, high = swap(from_y[..., :half, :], 1), swap(from_x[..., half:, :], 2)
        return part, from_x, from_y, low, high

    def reduce_far(blocks):
        return swap(blocks[3], 1), swap(blocks[4], 2)

    def reduce_near(blocks, far):
        half = feats // 2
        to_x, to_y = blocks[1], blocks[2]
        y_low = to_y[..., :half, :].astype(f32) + far[0].astype(f32)
        to_y = jnp.concatenate([y_low.astype(bf16), to_y[..., half:, :]], axis=-2)
        x_high = to_x[..., half:, :].astype(f32) + far[1].astype(f32)
        to_x = jnp.concatenate([to_x[..., :half, :], x_high.astype(bf16)], axis=-2)
        return swap(to_x, 1), swap(to_y, 2)

    def reduce_end(blocks, near):
        total = blocks[0].astype(f32) + near[0].astype(f32) + near[1].astype(f32)
        for bit in reversed(range(3, bits)):
            keep = total.shape[0] // 2
            total = total[:keep] + swap(total[keep:].astype(bf16), bit).astype(f32)
        return total[0]

    feat_ids = jnp.arange(width, dtype=jnp.int32)
    block_ids, within = feat_ids // feats, feat_ids % feats
    rel_at = 2 * (block_ids % (groups // 2)) + block_ids // (groups // 2)
    from_in = (g ^ rel_at) * feats + within
    rel_of = g ^ block_ids
    from_out = ((rel_of & 1) * (groups // 2) + (rel_of >> 1)) * feats + within

    def vectors_out(x):
        lead = x.shape[0]
        y = jnp.moveaxis(x.reshape((lead,) + (2,) * bits + (feats,)), 1, bits)
        for bit in range(bits):
            y = jnp.where((g >> bit) & 1 == 1, jnp.flip(y, bits - bit), y)
        return y.reshape(lead, width)

    slots = jnp.arange(groups, dtype=jnp.int32)
    places = jnp.arange(seq_deal.shape[0], dtype=jnp.int32)
    own_ids = device * groups + slots
    place_of = jnp.sum(jnp.where(own_ids[:, None] == seq_deal[None, :], places[None, :], 0), axis=1)
    target = place_of // groups // lanes
    source = jnp.sum(jnp.where(own_ids[:, None] == places[None, :], seq_deal[None, :], 0), axis=1) // groups // lanes
    rel_group = slots ^ g
    send_order = jnp.sum(jnp.where(target[None, :] == rel_group[:, None], slots[None, :], 0), axis=1)
    back_order = jnp.sum(jnp.where(source[None, :] == rel_group[:, None], slots[None, :], 0), axis=1)

    def exchange(pieces, order):
        for bit in order:
            view = pieces.reshape((groups >> (bit + 1), 2, (1 << bit) * piece_rows, width))
            got = swap(view[:, 1], bit)
            pieces = jnp.stack([view[:, 0], got], axis=1)
        return pieces.reshape(groups, piece_rows, width)

    def deal(x, order):
        sent = pick_pieces(x.reshape(groups, piece_rows, width), send_order)
        return turn_feats(pick_pieces(exchange(sent, order), source ^ g).reshape(rows, width), from_in)

    def undeal(x, order):
        sent = pick_pieces(turn_feats(x, from_out).reshape(groups, piece_rows, width), back_order)
        return pick_pieces(exchange(sent, order), target ^ g).reshape(rows, width)

    x_first = [1, 2] + list(range(3, bits)) + [0]
    y_first = [2, 1] + list(range(3, bits)) + [0]

    row_place = t * rows + jnp.arange(rows + halo, dtype=jnp.int32)
    begins = jnp.zeros_like(row_place)
    start = jnp.int32(0)
    for s in range(lengths.shape[1]):
        begins = jnp.where(row_place >= start, start, begins)
        start = start + lengths[0, s]
    off_ext = jnp.where(row_place < lanes * rows, row_place - begins, -1)[:, None]

    chan_count = kernel_bias.shape[0]
    small = jnp.concatenate(
        [kernel_taps.reshape(-1), kernel_bias, rate_bias, input_bias, decay_param, mixer_gain, feed_gain]
    )
    small = jnp.pad(small, (0, -small.shape[0] % 128))[None, None]
    step = 1
    while step < lanes:
        got = lax.ppermute(small, "tensor", [(i, i ^ step) for i in range(lanes)])
        small = jnp.concatenate([small, got], axis=0)
        step *= 2
    small = small.reshape(1, lanes, -1)
    for bit in range(bits):
        small = jnp.concatenate([small, swap(small, bit)], axis=0)

    x_low = deal(tokens, x_first)
    x = x_low.astype(f32)
    cot_low = deal(cotangent, y_first)

    def over_lanes(w):
        return lax.all_gather(w, "tensor", axis=0)

    lanes_x = over_lanes(recur_weight)
    lanes_y = over_lanes(gelu_weight)
    blocks = jnp.stack([jnp.swapaxes(rate_blocks, 1, 2), jnp.swapaxes(input_blocks, 1, 2)])
    blocks = lax.all_gather(after(blocks, lanes_x), "dp", axis=2, tiled=True)
    rate_t, input_t = blocks[0], blocks[1]
    lanes_o = over_lanes(flip_weight(mixer_out))
    cot_all = lax.all_gather(after(cot_low, lanes_o), "tensor", axis=0, tiled=True)

    def with_other(own):
        return own, swap(own, 0)

    part_g = gather_outer(feed_gate)
    part_x = gather_outer(lanes_x)
    part_y = gather_outer(lanes_y, part_g[3:])
    wx = with_other(join_lanes(*part_x))
    part_o = gather_outer(lanes_o, part_x[3:], cot_low)
    wg = with_other(join_feats(*part_g))
    wy = with_other(join_lanes(*part_y))
    wo = with_other(join_lanes(*part_o))

    chan_ids = jnp.arange(lru_total, dtype=jnp.int32)
    chan_lane, chan_dp, chan_in = chan_ids // chans, chan_ids % chans // chan_count, chan_ids % chan_count
    from_chan = ((chan_dp ^ g) * lanes + (chan_lane ^ t)) * chan_count + chan_in
    from_gain = (g ^ rel_at ^ g) * feats + within
    small_cols = 8 * chan_count
    chan_part = small[:, :, :small_cols].reshape(groups, lanes, 8, chan_count)
    chan_part = jnp.moveaxis(chan_part, 2, 0).reshape(8, lru_total)
    gain_part = small[:, 0, small_cols : small_cols + 2 * feats].reshape(groups, 2, feats)
    gain_part = jnp.swapaxes(gain_part, 0, 1).reshape(2, width)
    chan_vec = turn_feats(jnp.pad(chan_part, ((0, 8), (0, 0))), from_chan).astype(f32)
    gains = turn_feats(jnp.pad(gain_part, ((0, 14), (0, 0))), from_gain).astype(f32)
    gain_first, gain_second = gains[0], gains[1]
    vec = jnp.concatenate(
        [
            chan_vec[:7],
            jax.nn.softplus(-chan_vec[7:8]),
            jax.nn.sigmoid(-chan_vec[7:8]),
            jnp.zeros((7, lru_total), f32),
        ],
        axis=0,
    )

    normed_low = (x * inv_rms(x) * gain_first[None]).astype(bf16)
    normed_ext = jnp.concatenate([up(normed_low[rows - halo :]), normed_low], axis=0)
    bx_ext = rows_into(normed_ext, wx)
    part_u = gather_outer(feed_up, part_y[3:], bx_ext)
    by = rows_into(normed_low, wy)
    conv_low, state_loc, prod_loc = mix_fwd(bx_ext, off_ext, vec, rate_t, input_t)
    part_d = gather_outer(flip_weight(feed_down), part_o[3:], state_loc)
    wu = with_other(join_feats(*part_u))
    wd = with_other(join_feats(*part_d))
    edge = jnp.concatenate([state_loc[rows - 1 :], prod_loc[rows - 1 :], jnp.zeros((6, lru_total), f32)], axis=0)

    def carry_in(edge, direction):
        total = jnp.zeros((1, lru_total), f32)
        factor = jnp.ones((1, lru_total), f32)
        for by_lanes in range(1, lanes):
            far = shift(edge, direction * by_lanes)
            total = total + factor * far[0:1]
            factor = factor * far[1:2]
        return jnp.broadcast_to(total, (8, lru_total))

    enter = carry_in(edge, 1)
    state, mixed = mix_out(state_loc, prod_loc, enter, by, wide)
    middle = x + rows_back([(mixed, wo)])
    ns_low = (middle * inv_rms(middle) * gain_second[None]).astype(bf16)
    ns_rows = [ns_low]
    for _ in range(lanes - 1):
        ns_rows.append(up(ns_rows[-1]))

    pair = 2
    hidden, g_gate, g_up = [], [], []
    total = None
    for at in range(0, lanes, pair):
        first = ns_rows[at] if total is None else after(ns_rows[at], total)
        h, gg, gu = feed_pair([first] + ns_rows[at + 1 : at + pair], cot_all, at, wg, wu, wd, lane, lanes)
        hidden.append(h)
        g_gate.append(gg)
        g_up.append(gu)
        if total is None:
            total = feed_back([(gg, wg), (gu, wu)], 1, rows, [], bf16)

    def other_half(lefts, rights, *deps, **kind):
        first = after(rights[0], *deps) if deps else rights[0]
        return weight_grad(lefts, [first] + rights[1:], 1, feats, lane, lanes, **kind)

    def own_half(lefts, rights, other, *deps, **kind):
        first = after(rights[0], *deps) if deps else rights[0]
        return weight_grad(lefts, [first] + rights[1:], 0, feats, lane, lanes, got=swap(other, 0), **kind)

    def second_part(k, total, *deps):
        terms = [(after(g_gate[k // pair], *deps) if deps else g_gate[k // pair], wg), (g_up[k // pair], wu)]
        return feed_back(terms, k % pair, rows, [] if total is None else [up(total)], f32 if k == 0 else bf16)

    cot_parts = [(cot_all, rows, k) for k in range(lanes)]
    for k in range(2, lanes - 2):
        total = second_part(k, total)
    total = second_part(lanes - 2, total)
    other_down = other_half(cot_parts, hidden, total)
    other_gate = other_half(ns_rows, g_gate, other_down)
    own_down = own_half(cot_parts, hidden, other_down, other_gate)
    far_down = reduce_far(own_down)
    own_gate = own_half(ns_rows, g_gate, other_gate, own_down)
    far_gate = reduce_far(own_gate)
    total = second_part(lanes - 1, total, own_gate, far_down)
    near_down = reduce_near(own_down, far_down)
    other_up = other_half(ns_rows, g_up, total)
    near_gate = reduce_near(own_gate, far_gate)
    own_up = own_half(ns_rows, g_up, other_up, far_gate)
    far_up = reduce_far([after(b, near_down) for b in own_up])
    g_second = second_part(0, total, own_up, near_down)
    near_up = reduce_near(own_up, far_up)

    g_mid_part, d_gain_second = norm_back(middle, gain_second[None], g_second)
    g_middle = cot_low.astype(f32) + g_mid_part
    g1 = g_middle.astype(bf16)

    def lane_sum(blocks):
        return lax.psum_scatter(blocks.astype(bf16), "tensor", scatter_dimension=0).astype(f32)

    by_lane = dict(by_lane=True)
    other_out = other_half([g1], [mixed], **by_lane)
    gm = rows_into(after(g1, other_out, near_gate), wo)
    own_out = own_half([g1], [mixed], other_out, gm, far_up, **by_lane)
    far_out = reduce_far(own_out)
    gy_low, adj_loc, tail, edge_back = mix_adj(after(gm, own_out), by, state, conv_low, off_ext, vec, rate_t)
    hand = carry_in(edge_back, -1)
    other_y = other_half([normed_low], [gy_low], near_up, **by_lane)
    near_out = reduce_near(own_out, far_out)
    feed_sum = feed_out([after(hidden[0], other_y, far_out)] + hidden[1:], wd, lane, lanes)
    feed_sum = lax.psum_scatter(feed_sum, "tensor", scatter_dimension=0, tiled=True)
    own_y = own_half([normed_low], [gy_low], other_y, **by_lane)
    far_y = reduce_far(own_y)
    g_conv, d_rate, d_input, sums_gate = mix_bwd(
        after(adj_loc, own_y), tail, hand, state, enter, conv_low, off_ext, vec, rate_t, input_t
    )
    gc_next = lax.ppermute(g_conv[:halo], "tensor", [(i, (i - 1) % lanes) for i in range(lanes)])
    gx_low, sums_conv = conv_bwd(g_conv, gc_next, bx_ext, off_ext, vec, wide)
    near_y = reduce_near(own_y, far_y)
    other_x = other_half([normed_low], [gx_low], near_out, **by_lane)
    g_first = rows_back([(after(gx_low, other_x), wx), (gy_low, wy)])
    own_x = own_half([normed_low], [gx_low], other_x, far_y, **by_lane)
    far_x = reduce_far(own_x)
    d_down = reduce_end(own_down, near_down)
    d_gate = reduce_end(own_gate, near_gate)
    d_up = reduce_end(own_up, near_up)
    d_out = lane_sum(reduce_end(own_out, near_out))
    near_x = reduce_near(own_x, far_x)
    d_y = lane_sum(reduce_end(own_y, near_y))
    d_x = lane_sum(reduce_end(own_x, near_x))
    g_tok_part, d_gain_first = norm_back(x, gain_first[None], g_first)
    tokens_grad = undeal((g_middle + g_tok_part).astype(bf16), y_first)
    block_out = undeal((middle + feed_sum.astype(f32)).astype(bf16), x_first)

    d_blocks = lax.psum_scatter(jnp.stack([d_rate, d_input]), "dp", scatter_dimension=2, tiled=True)
    d_blocks = jnp.swapaxes(lax.psum(d_blocks, "tensor"), 2, 3).astype(f32)
    d_gains = vectors_out(jnp.stack([d_gain_first, d_gain_second]))
    vectors = jnp.concatenate([sums_conv[:5], sums_gate[:3], d_gains, jnp.zeros((6, width), f32)], axis=0)
    for bit in range(bits):
        vectors = vectors + swap(vectors, bit)
    step = 1
    while step < lanes:
        vectors = vectors + lax.ppermute(vectors, "tensor", [(i, i ^ step) for i in range(lanes)])
        step *= 2
    chan_grad = lax.dynamic_slice_in_dim(vectors[:8], (t * groups + g) * chan_count, chan_count, axis=1)
    gain_grad = lax.dynamic_slice_in_dim(vectors[8:10], g * feats, feats, axis=1)

    return (
        block_out,
        tokens_grad,
        gain_grad[0],
        d_x,
        d_y,
        chan_grad[0:4],
        chan_grad[4],
        chan_grad[5],
        chan_grad[6],
        chan_grad[7],
        d_blocks[0],
        d_blocks[1],
        d_out.T,
        gain_grad[1],
        d_gate,
        d_up,
        d_down.T,
    )


def solution(mesh):
    rows = P(("dp", "tensor"), None)
    feat = P("dp")
    chan = P(("tensor", "dp"))
    taps = P(None, ("tensor", "dp"))
    into = P("dp", "tensor")
    back = P("tensor", "dp")
    blocks = P(None, None, "dp")
    in_specs = (
        rows, rows, P("dp", None), P(), feat, into, into, taps, chan, chan, chan, chan, blocks, blocks, back, feat,
        into, into, back,
    )
    out_specs = (
        rows, rows, feat, into, into, taps, chan, chan, chan, chan, blocks, blocks, back, feat, into, into, back,
    )
    return jax.shard_map(per_device, mesh=mesh, in_specs=in_specs, out_specs=out_specs, check_vma=False)
```

```python
import functools

import jax
import jax.numpy as jnp
from jax import lax
from jax.experimental import pallas as pl
from jax.experimental.pallas import tpu as pltpu
from jax.sharding import PartitionSpec as P

norm_eps = 1e-06
scale_floor = 0.001
halo = 8
bf16 = jnp.bfloat16
f32 = jnp.float32
gelu_c = 0.7978845608028654
gelu_k = 0.044715


def gelu_both(x):
    sq = x * x
    th = jnp.tanh(gelu_c * x * (1.0 + gelu_k * sq))
    half = 0.5 * (1.0 + th)
    return x * half, half + 0.5 * x * (1.0 - th * th) * gelu_c * (1.0 + 3.0 * gelu_k * sq)


def inv_rms(x):
    return lax.rsqrt(jnp.mean(x * x, axis=-1, keepdims=True) + norm_eps)


def norm_back(x, gain, grad):
    r = inv_rms(x)
    v = gain * grad
    dx = r * v - x * (r * r * r) * jnp.mean(x * v, axis=-1, keepdims=True)
    return dx, jnp.sum(grad * x * r, axis=0)


def mm(a, b):
    return jnp.dot(a, b, preferred_element_type=f32)


def mm_nt(a, b):
    return lax.dot_general(a, b, (((1,), (1,)), ((), ())), preferred_element_type=f32)


def mm_tn(a, b):
    return lax.dot_general(a, b, (((0,), (0,)), ((), ())), preferred_element_type=f32)


roomy = pltpu.CompilerParams(vmem_limit_bytes=56 * 1024 * 1024)


def cost(microseconds):
    return pl.CostEstimate(flops=int(microseconds * 1.15e9), bytes_accessed=1024, transcendentals=0)


def tile_of(total, most):
    for tile in range(most - most % 128, 0, -128):
        if total % tile == 0:
            return tile
    return total


def _pick_kernel(order_ref, x_ref, o_ref):
    for i in range(o_ref.shape[0]):
        o_ref[i] = x_ref[order_ref[i]]


def pick_pieces(pieces, order):
    return pl.pallas_call(
        _pick_kernel,
        in_specs=[pl.BlockSpec(memory_space=pltpu.SMEM), pl.BlockSpec(memory_space=pltpu.VMEM)],
        out_specs=pl.BlockSpec(memory_space=pltpu.VMEM),
        out_shape=jax.ShapeDtypeStruct(pieces.shape, pieces.dtype),
        name="pick_pieces", cost_estimate=cost(2),
    )(order, pieces)


def _turn_kernel(from_ref, x_ref, o_ref):
    width = x_ref.shape[1]
    place = lax.broadcasted_iota(jnp.int32, (width, o_ref.shape[1]), 0)
    hot = jnp.where(place == from_ref[...], 1.0, 0.0).astype(bf16)
    o_ref[...] = mm(x_ref[...], hot).astype(bf16)


def turn_feats(x, from_feat):
    rows, width = x.shape
    tile = tile_of(width, 512)
    return pl.pallas_call(
        _turn_kernel,
        grid=(width // tile,),
        in_specs=[pl.BlockSpec((1, tile), lambda j: (0, j)), pl.BlockSpec((rows, width), lambda j: (0, 0))],
        out_specs=pl.BlockSpec((rows, tile), lambda j: (0, j)),
        out_shape=jax.ShapeDtypeStruct(x.shape, bf16),
        compiler_params=roomy,
        name="turn_feats", cost_estimate=cost(6),
    )(from_feat[None], x)


def unit(n):
    one = lax.broadcasted_iota(jnp.int32, (n, n), 0) == lax.broadcasted_iota(jnp.int32, (n, n), 1)
    return jnp.where(one, 1.0, 0.0).astype(bf16)


def _flip_kernel(x_ref, o_ref):
    o_ref[...] = mm_tn(x_ref[...], unit(x_ref.shape[0])).astype(bf16)


def flip_weight(x):
    rows, cols = x.shape
    tile = tile_of(rows, 640)
    return pl.pallas_call(
        _flip_kernel,
        grid=(rows // tile,),
        in_specs=[pl.BlockSpec((tile, cols), lambda j: (j, 0))],
        out_specs=pl.BlockSpec((cols, tile), lambda j: (0, j)),
        out_shape=jax.ShapeDtypeStruct((cols, rows), bf16),
        compiler_params=roomy,
        name="flip_weight", cost_estimate=cost(4),
    )(x)


def _join_kernel(own_ref, x_ref, y_ref, low_ref, high_ref, out_ref):
    extra, feats = own_ref.shape[0], own_ref.shape[1]
    half = feats // 2
    for e in range(extra):
        for q, ref in enumerate((own_ref, x_ref, y_ref)):
            out_ref[(4 * e + q) * feats : (4 * e + q + 1) * feats] = ref[e]
        at = (4 * e + 3) * feats
        out_ref[at : at + half] = low_ref[e]
        out_ref[at + half : at + feats] = high_ref[e]


def join_feats(own, from_x, from_y, low, high):
    extra, feats, cols = own.shape
    tile = tile_of(cols, 640)
    full = pl.BlockSpec((extra, feats, tile), lambda j: (0, 0, j))
    part = pl.BlockSpec((extra, feats // 2, tile), lambda j: (0, 0, j))
    rows = extra * 4 * feats
    return pl.pallas_call(
        _join_kernel,
        grid=(cols // tile,),
        in_specs=[full, full, full, part, part],
        out_specs=pl.BlockSpec((rows, tile), lambda j: (0, j)),
        out_shape=jax.ShapeDtypeStruct((rows, cols), bf16),
        compiler_params=roomy,
        name="join_feats", cost_estimate=cost(5.5),
    )(own, from_x, from_y, low, high)


def _join_lanes_kernel(own_ref, x_ref, y_ref, low_ref, high_ref, out_ref):
    extra, feats = own_ref.shape[0], own_ref.shape[2]
    half = feats // 2
    for e in range(extra):
        for q, ref in enumerate((own_ref, x_ref, y_ref)):
            out_ref[0, (4 * e + q) * feats : (4 * e + q + 1) * feats] = ref[e, 0]
        at = (4 * e + 3) * feats
        out_ref[0, at : at + half] = low_ref[e, 0]
        out_ref[0, at + half : at + feats] = high_ref[e, 0]


def join_lanes(own, from_x, from_y, low, high):
    extra, lanes, feats, chans = own.shape
    full = pl.BlockSpec((extra, 1, feats, chans), lambda k: (0, k, 0, 0))
    part = pl.BlockSpec((extra, 1, feats // 2, chans), lambda k: (0, k, 0, 0))
    rows = extra * 4 * feats
    return pl.pallas_call(
        _join_lanes_kernel,
        grid=(lanes,),
        in_specs=[full, full, full, part, part],
        out_specs=pl.BlockSpec((1, rows, chans), lambda k: (k, 0, 0)),
        out_shape=jax.ShapeDtypeStruct((lanes, rows, chans), bf16),
        compiler_params=roomy,
        name="join_lanes",
        cost_estimate=cost(5),
    )(own, from_x, from_y, low, high)


def chan_spec(rows, chans):
    if chans % 128 == 0:
        return pl.BlockSpec((rows, chans), lambda k: (0, k))
    return pl.BlockSpec((1, rows, chans), lambda k: (k, 0, 0))


def chan_in(x, chans):
    if chans % 128 == 0:
        return x
    return jnp.swapaxes(x.reshape(x.shape[0], -1, chans), 0, 1)


def chan_get(ref):
    return ref[...] if len(ref.shape) == 2 else ref[0]


def rows_into(a, weight):
    rows, width = a.shape
    lanes, half, chans = weight[0].shape
    flat = chans % 128 == 0

    def kernel(a_ref, own_ref, other_ref, out_ref):
        got = mm(a_ref[:, :half], own_ref[0]) + mm(a_ref[:, half:], other_ref[0])
        if flat:
            out_ref[...] = got
        else:
            out_ref[0] = got

    block = pl.BlockSpec((1, half, chans), lambda k: (k, 0, 0))
    out = pl.pallas_call(
        kernel,
        grid=(lanes,),
        in_specs=[pl.BlockSpec((rows, width), lambda k: (0, 0)), block, block],
        out_specs=chan_spec(rows, chans),
        out_shape=jax.ShapeDtypeStruct((rows, lanes * chans) if flat else (lanes, rows, chans), f32),
        compiler_params=roomy,
        name="rows_into",
        cost_estimate=cost(11),
    )(a, *weight)
    return out if flat else jnp.swapaxes(out, 0, 1).reshape(rows, lanes * chans)


def rows_back(terms):
    rows = terms[0][0].shape[0]
    lanes, half, chans = terms[0][1][0].shape
    pairs = len(terms)

    def kernel(*refs):
        out_ref = refs[-1]

        @pl.when(pl.program_id(0) == 0)
        def _():
            out_ref[...] = jnp.zeros_like(out_ref)

        for side in range(2):
            total = None
            for p in range(pairs):
                part = mm_nt(chan_get(refs[p]), refs[pairs + 2 * p + side][0])
                total = part if total is None else total + part
            cols = slice(side * half, (side + 1) * half)
            out_ref[:, cols] = out_ref[:, cols] + total

    block = pl.BlockSpec((1, half, chans), lambda k: (k, 0, 0))
    arrays = [chan_in(b, chans) for b, _ in terms]
    for _, weight in terms:
        arrays += list(weight)
    return pl.pallas_call(
        kernel,
        grid=(lanes,),
        in_specs=[chan_spec(rows, chans)] * pairs + [block] * (2 * pairs),
        out_specs=pl.BlockSpec((rows, 2 * half), lambda k: (0, 0)),
        out_shape=jax.ShapeDtypeStruct((rows, 2 * half), f32),
        compiler_params=roomy,
        name="rows_back",
        cost_estimate=cost(8 * pairs + 3),
    )(*arrays)


def lane_block(lane, k, lanes):
    return lax.rem(lane[0] - k + lanes, lanes)


def feed_pair(ns, cot_all, at, gate, up, down, lane, lanes):
    count = len(ns)
    rows, width = ns[0].shape
    half, hidden = gate[0].shape
    tile = tile_of(hidden, 640)

    def kernel(lane_ref, *refs):
        ns_refs, cot_refs = refs[:count], refs[count : 2 * count]
        weights = refs[2 * count : 2 * count + 6]
        hid_ref, gate_ref, up_ref, ns_all, cot_rows = refs[2 * count + 6 :]

        @pl.when(pl.program_id(0) == 0)
        def _():
            for i in range(count):
                ns_all[i * rows : (i + 1) * rows] = ns_refs[i][...]
                cot_rows[i * rows : (i + 1) * rows] = cot_refs[i][...]

        def times(a, i):
            return mm(a[:, :half], weights[i][...]) + mm(a[:, half:], weights[i + 1][...])

        act, slope = gelu_both(times(ns_all, 0))
        up_pre = times(ns_all, 2)
        hid_ref[...] = (act * up_pre).astype(bf16)
        grad = times(cot_rows, 4)
        gate_ref[...] = (grad * up_pre * slope).astype(bf16)
        up_ref[...] = (grad * act).astype(bf16)

    whole = pl.BlockSpec((rows, width), lambda j, lane: (0, 0))
    cots = [
        pl.BlockSpec((rows, width), functools.partial(lambda j, lane, k: (lane_block(lane, k, lanes), 0), k=at + i))
        for i in range(count)
    ]
    piece = pl.BlockSpec((half, tile), lambda j, lane: (0, j))
    out = pl.BlockSpec((count * rows, tile), lambda j, lane: (0, j))
    return pl.pallas_call(
        kernel,
        grid_spec=pltpu.PrefetchScalarGridSpec(
            num_scalar_prefetch=1,
            grid=(hidden // tile,),
            in_specs=[whole] * count + cots + [piece] * 6,
            out_specs=[out] * 3,
            scratch_shapes=[pltpu.VMEM((count * rows, width), bf16)] * 2,
        ),
        out_shape=[jax.ShapeDtypeStruct((count * rows, hidden), bf16)] * 3,
        compiler_params=roomy,
        name="feed_pair",
        cost_estimate=cost(27),
    )(lane, *ns, *([cot_all] * count), *gate, *up, *down)


def feed_back(terms, at, rows, adds, kind):
    half, hidden = terms[0][1][0].shape
    width = 2 * half
    tile = tile_of(half, 640)
    steps = half // tile
    pairs = len(terms)

    def kernel(*refs):
        out_ref = refs[-1]
        j = pl.program_id(0)
        for side in range(2):

            @pl.when((j < steps) if side == 0 else (j >= steps))
            def _():
                total = None
                for p in range(pairs):
                    part = mm_nt(refs[p][...], refs[pairs + 2 * p + side][...])
                    total = part if total is None else total + part
                for extra_ref in refs[3 * pairs : -1]:
                    total = total + extra_ref[...].astype(f32)
                out_ref[...] = total.astype(kind)

    specs = [pl.BlockSpec((rows, hidden), lambda j: (at, 0))] * pairs
    arrays = [b for b, _ in terms]
    for _, weight in terms:
        specs.append(pl.BlockSpec((tile, hidden), lambda j: (jnp.minimum(j, steps - 1), 0)))
        specs.append(pl.BlockSpec((tile, hidden), lambda j: (jnp.maximum(j - steps, 0), 0)))
        arrays += list(weight)
    specs += [pl.BlockSpec((rows, tile), lambda j: (0, j))] * len(adds)
    return pl.pallas_call(
        kernel,
        grid=(2 * steps,),
        in_specs=specs,
        out_specs=pl.BlockSpec((rows, tile), lambda j: (0, j)),
        out_shape=jax.ShapeDtypeStruct((rows, width), kind),
        compiler_params=roomy,
        name="feed_back",
        cost_estimate=cost(13),
    )(*arrays, *adds)


def feed_out(hidden, weight, lane, lanes):
    half, units = weight[0].shape
    width = 2 * half
    tile = tile_of(half, 640)
    steps = half // tile
    many = len(hidden)
    count = lanes // many
    rows = hidden[0].shape[0] // count

    def kernel(lane_ref, *refs):
        out_ref = refs[-1]
        j = pl.program_id(0)
        for side in range(2):

            @pl.when((j < steps) if side == 0 else (j >= steps))
            def _():
                for i in range(many):
                    got = mm_nt(refs[i][...], refs[many + side][...]).astype(bf16)
                    for c in range(count):
                        at = lane_block(lane_ref, i * count + c, lanes) * rows
                        out_ref[pl.ds(pl.multiple_of(at, rows), rows)] = got[c * rows : (c + 1) * rows]

    whole = pl.BlockSpec((count * rows, units), lambda j, lane: (0, 0))
    return pl.pallas_call(
        kernel,
        grid_spec=pltpu.PrefetchScalarGridSpec(
            num_scalar_prefetch=1,
            grid=(2 * steps,),
            in_specs=[whole] * many
            + [
                pl.BlockSpec((tile, units), lambda j, lane: (jnp.minimum(j, steps - 1), 0)),
                pl.BlockSpec((tile, units), lambda j, lane: (jnp.maximum(j - steps, 0), 0)),
            ],
            out_specs=pl.BlockSpec((lanes * rows, tile), lambda j, lane: (0, j)),
        ),
        out_shape=jax.ShapeDtypeStruct((lanes * rows, width), bf16),
        compiler_params=roomy,
        name="feed_out",
        cost_estimate=cost(18),
    )(lane, *hidden, *weight)


def weight_grad(lefts, rights, side, feats, lane, lanes, got=None, by_lane=False):
    specs, arrays = [], []
    for left in lefts:
        if isinstance(left, tuple):
            array, left_rows, k = left
            pick = functools.partial(lambda j, lane, k: (lane_block(lane, k, lanes), side), k=k)
        else:
            array, left_rows, pick = left, left.shape[0], lambda j, lane: (0, side)
        half = array.shape[1] // 2
        specs.append(pl.BlockSpec((left_rows, half), pick))
        arrays.append(array)
    count = len(lefts)
    right_rows, cols = rights[0].shape
    many = len(rights)
    tile = cols // lanes if by_lane else tile_of(cols, 640)
    extra = half // (4 * feats)
    part = feats // 2

    def kernel(lane_ref, *refs):
        left_refs, right_refs = refs[:count], refs[count : count + many]
        rest = refs[count + many :]
        if count > 1:
            all_ref, rest = rest[-1], rest[:-1]

            @pl.when(pl.program_id(0) == 0)
            def _():
                for i in range(count):
                    all_ref[i * left_rows : (i + 1) * left_rows] = left_refs[i][...]
        else:
            all_ref = left_refs[0]
        total = None
        for i in range(many):
            piece = mm_tn(all_ref[i * right_rows : (i + 1) * right_rows], chan_get(right_refs[i]))
            total = piece if total is None else total + piece
        if got is None:
            if by_lane:
                rest[0][0] = total.astype(bf16)
            else:
                rest[0][...] = total.astype(bf16)
            return
        total = (total + chan_get(rest[0]).astype(f32)).astype(bf16)
        cuts = (0, feats, 2 * feats, 3 * feats, 3 * feats + part, 4 * feats)
        for e in range(extra):
            base = 4 * feats * e
            for ref, a, b in zip(rest[1:], cuts[:-1], cuts[1:]):
                if by_lane:
                    ref[e, 0] = total[base + a : base + b]
                else:
                    ref[e] = total[base + a : base + b]

    flat = not by_lane or tile % 128 == 0
    if flat:
        right_spec = pl.BlockSpec((right_rows, tile), lambda j, lane: (0, j))
    else:
        right_spec = pl.BlockSpec((1, right_rows, tile), lambda j, lane: (j, 0, 0))
        rights = [chan_in(r, tile) for r in rights]
    if by_lane:
        sent, sent_shape = pl.BlockSpec((1, half, tile), lambda j, lane: (j, 0, 0)), (lanes, half, tile)
        block = lambda n: pl.BlockSpec((extra, 1, n, tile), lambda j, lane: (0, j, 0, 0))
        block_shape = lambda n: (extra, lanes, n, tile)
    else:
        sent, sent_shape = pl.BlockSpec((half, tile), lambda j, lane: (0, j)), (half, cols)
        block = lambda n: pl.BlockSpec((extra, n, tile), lambda j, lane: (0, 0, j))
        block_shape = lambda n: (extra, n, cols)
    sizes = (feats, feats, feats, part, part)
    specs += [right_spec] * many
    arrays += list(rights)
    if got is None:
        out_specs, out_shape = sent, jax.ShapeDtypeStruct(sent_shape, bf16)
    else:
        specs.append(sent)
        arrays.append(got)
        out_specs = [block(n) for n in sizes]
        out_shape = [jax.ShapeDtypeStruct(block_shape(n), bf16) for n in sizes]
    return pl.pallas_call(
        kernel,
        grid_spec=pltpu.PrefetchScalarGridSpec(
            num_scalar_prefetch=1,
            grid=(cols // tile,),
            in_specs=specs,
            out_specs=out_specs,
            scratch_shapes=[pltpu.VMEM((left_rows * count, half), bf16)] if count > 1 else [],
        ),
        out_shape=out_shape,
        compiler_params=roomy,
        name="weight_grad",
        cost_estimate=cost(10 if count > 1 else 7),
    )(lane, *arrays)


def scan_rows(a, b, reverse):
    rows = a.shape[0]
    place = lax.broadcasted_iota(jnp.int32, a.shape, 0)
    step = 1
    while step < rows:
        if reverse:
            inside = place < rows - step
            turn = rows - step
        else:
            inside = place >= step
            turn = step
        a_far = jnp.where(inside, pltpu.roll(a, turn, 0), 1.0)
        b_far = jnp.where(inside, pltpu.roll(b, turn, 0), 0.0)
        b = a * b_far + b
        a = a * a_far
        step *= 2
    return a, b


def gate_values(conv_low, rate_t, input_t, vec, first):
    q = jax.nn.sigmoid(mm_nt(conv_low, rate_t) + vec[5:6])
    p = jax.nn.sigmoid(mm_nt(conv_low, input_t) + vec[6:7])
    decay = jnp.where(first, 0.0, jnp.exp(-8.0 * q * vec[7:8]))
    room = 1.0 - decay * decay
    scale = jnp.sqrt(jnp.maximum(room, scale_floor))
    return q, p, decay, room, scale


def _mix_fwd_kernel(bx_ref, off_ref, vec_ref, rate_ref, input_ref, conv_ref, state_ref, prod_ref):
    rows = conv_ref.shape[0]
    off = off_ref[0:rows]
    vec = vec_ref[...]
    conv = jnp.broadcast_to(vec[4:5], state_ref.shape)
    for lag in range(4):
        conv = conv + jnp.where(off >= lag, bx_ref[halo - lag : halo - lag + rows], 0.0) * vec[lag : lag + 1]
    conv_low = conv.astype(bf16)
    conv_ref[...] = conv_low
    q, p, decay, room, scale = gate_values(conv_low, rate_ref[0], input_ref[0], vec, off == 0)
    driven = scale * p * conv_low.astype(f32)
    prod, state = scan_rows(decay, driven, False)
    state_ref[...] = state
    prod_ref[...] = prod


def mix_fwd(bx_ext, off_ext, vec, rate_t, input_t):
    heads, width, _ = rate_t.shape
    ext = bx_ext.shape[0]
    rows = ext - halo
    col = lambda h: (0, h)
    return pl.pallas_call(
        _mix_fwd_kernel,
        grid=(heads,),
        in_specs=[
            pl.BlockSpec((ext, width), col),
            pl.BlockSpec((ext, 1), lambda h: (0, 0)),
            pl.BlockSpec((16, width), col),
            pl.BlockSpec((1, width, width), lambda h: (h, 0, 0)),
            pl.BlockSpec((1, width, width), lambda h: (h, 0, 0)),
        ],
        out_specs=[pl.BlockSpec((rows, width), col)] * 3,
        out_shape=[
            jax.ShapeDtypeStruct((rows, heads * width), bf16),
            jax.ShapeDtypeStruct((rows, heads * width), f32),
            jax.ShapeDtypeStruct((rows, heads * width), f32),
        ],
        name="mix_fwd", cost_estimate=cost(12),
    )(bx_ext, off_ext, vec, rate_t, input_t)


def _mix_out_kernel(state_ref, prod_ref, enter_ref, by_ref, full_ref, mixed_ref):
    state = state_ref[...] + prod_ref[...] * enter_ref[0:1]
    full_ref[...] = state
    act, _ = gelu_both(by_ref[...])
    mixed_ref[...] = (state * act).astype(bf16)


def mix_out(state, prod, enter, by, width):
    rows, total = state.shape
    blk = pl.BlockSpec((rows, width), lambda h: (0, h))
    return pl.pallas_call(
        _mix_out_kernel,
        grid=(total // width,),
        in_specs=[blk, blk, pl.BlockSpec((8, width), lambda h: (0, h)), blk],
        out_specs=[blk, blk],
        out_shape=[jax.ShapeDtypeStruct((rows, total), f32), jax.ShapeDtypeStruct((rows, total), bf16)],
        name="mix_out", cost_estimate=cost(6),
    )(state, prod, enter, by)


def _mix_adj_kernel(gm_ref, by_ref, full_ref, conv_ref, off_ref, vec_ref, rate_ref, gy_ref, adj_ref, tail_ref, edge_ref):
    rows = conv_ref.shape[0]
    vec = vec_ref[...]
    off = off_ref[0:rows]
    q = jax.nn.sigmoid(mm_nt(conv_ref[...], rate_ref[0]) + vec[5:6])
    decay = jnp.where(off == 0, 0.0, jnp.exp(-8.0 * q * vec[7:8]))
    act, act_grad = gelu_both(by_ref[...])
    gm = gm_ref[...]
    gy_ref[...] = (gm * full_ref[...] * act_grad).astype(bf16)
    place = lax.broadcasted_iota(jnp.int32, decay.shape, 0)
    after = jnp.where(place == rows - 1, 1.0, pltpu.roll(decay, rows - 1, 0))
    tail, adj = scan_rows(after, gm * act, True)
    adj_ref[...] = adj
    tail_ref[...] = tail
    edge_ref[0:1] = decay[0:1] * adj[0:1]
    edge_ref[1:2] = decay[0:1] * tail[0:1]
    edge_ref[2:8] = jnp.zeros((6, decay.shape[1]), f32)


def mix_adj(gm, by, full, conv, off_ext, vec, rate_t):
    heads, width, _ = rate_t.shape
    rows, total = gm.shape
    blk = pl.BlockSpec((rows, width), lambda h: (0, h))
    return pl.pallas_call(
        _mix_adj_kernel,
        grid=(heads,),
        in_specs=[
            blk,
            blk,
            blk,
            blk,
            pl.BlockSpec((rows + halo, 1), lambda h: (0, 0)),
            pl.BlockSpec((16, width), lambda h: (0, h)),
            pl.BlockSpec((1, width, width), lambda h: (h, 0, 0)),
        ],
        out_specs=[blk, blk, blk, pl.BlockSpec((8, width), lambda h: (0, h))],
        out_shape=[
            jax.ShapeDtypeStruct((rows, total), bf16),
            jax.ShapeDtypeStruct((rows, total), f32),
            jax.ShapeDtypeStruct((rows, total), f32),
            jax.ShapeDtypeStruct((8, total), f32),
        ],
        name="mix_adj", cost_estimate=cost(13),
    )(gm, by, full, conv, off_ext, vec, rate_t)


def _mix_bwd_kernel(
    adj_ref, tail_ref, hand_ref, full_ref, enter_ref, conv_ref, off_ref, vec_ref, rate_ref, input_ref,
    gc_ref, drate_ref, dinput_ref, sums_ref,
):
    rows = conv_ref.shape[0]
    vec = vec_ref[...]
    off = off_ref[0:rows]
    conv_low = conv_ref[...]
    conv = conv_low.astype(f32)
    rate_t, input_t = rate_ref[0], input_ref[0]
    q, p, decay, room, scale = gate_values(conv_low, rate_t, input_t, vec, off == 0)
    adj = adj_ref[...] + tail_ref[...] * hand_ref[0:1]
    place = lax.broadcasted_iota(jnp.int32, adj.shape, 0)
    before = jnp.where(place == 0, enter_ref[0:1], pltpu.roll(full_ref[...], 1, 0))
    g_decay = adj * before - jnp.where(room > scale_floor, adj * p * conv * decay / scale, 0.0)
    g_log = g_decay * decay
    g_rate = (-8.0 * g_log * vec[7:8] * q * (1.0 - q)).astype(bf16)
    g_input = (adj * scale * conv * p * (1.0 - p)).astype(bf16)
    gc_ref[...] = adj * scale * p + mm(g_rate, rate_t) + mm(g_input, input_t)
    drate_ref[0] = mm_tn(g_rate, conv_low).astype(bf16)
    dinput_ref[0] = mm_tn(g_input, conv_low).astype(bf16)
    sums_ref[0:1] = jnp.sum(8.0 * g_log * q, axis=0, keepdims=True) * vec[8:9]
    sums_ref[1:2] = jnp.sum(g_rate.astype(f32), axis=0, keepdims=True)
    sums_ref[2:3] = jnp.sum(g_input.astype(f32), axis=0, keepdims=True)
    sums_ref[3:8] = jnp.zeros((5, adj.shape[1]), f32)


def mix_bwd(adj, tail, hand, full, enter, conv, off_ext, vec, rate_t, input_t):
    heads, width, _ = rate_t.shape
    rows, total = adj.shape
    col = lambda h: (0, h)
    blk = pl.BlockSpec((rows, width), col)
    row8 = pl.BlockSpec((8, width), col)
    square = pl.BlockSpec((1, width, width), lambda h: (h, 0, 0))
    return pl.pallas_call(
        _mix_bwd_kernel,
        grid=(heads,),
        in_specs=[
            blk, blk, row8, blk, row8, blk,
            pl.BlockSpec((rows + halo, 1), lambda h: (0, 0)),
            pl.BlockSpec((16, width), col),
            square, square,
        ],
        out_specs=[blk, square, square, row8],
        out_shape=[
            jax.ShapeDtypeStruct((rows, total), f32),
            jax.ShapeDtypeStruct((heads, width, width), bf16),
            jax.ShapeDtypeStruct((heads, width, width), bf16),
            jax.ShapeDtypeStruct((8, total), f32),
        ],
        name="mix_bwd", cost_estimate=cost(14),
    )(adj, tail, hand, full, enter, conv, off_ext, vec, rate_t, input_t)


def _conv_bwd_kernel(gc_ref, next_ref, bx_ref, off_ref, vec_ref, gx_ref, sums_ref, ext_ref):
    rows = gc_ref.shape[0]
    vec = vec_ref[...]
    gc = gc_ref[...]
    ext_ref[0:rows] = gc
    ext_ref[rows : rows + halo] = next_ref[...]
    off = off_ref[0:rows]
    gx = gc * vec[0:1]
    sums_ref[0:1] = jnp.sum(gc * bx_ref[halo : halo + rows], axis=0, keepdims=True)
    for lag in range(1, 4):
        gx = gx + jnp.where(off_ref[lag : lag + rows] >= lag, ext_ref[lag : lag + rows], 0.0) * vec[lag : lag + 1]
        term = jnp.where(off >= lag, gc * bx_ref[halo - lag : halo - lag + rows], 0.0)
        sums_ref[lag : lag + 1] = jnp.sum(term, axis=0, keepdims=True)
    sums_ref[4:5] = jnp.sum(gc, axis=0, keepdims=True)
    sums_ref[5:8] = jnp.zeros((3, gc.shape[1]), f32)
    gx_ref[...] = gx.astype(bf16)


def conv_bwd(gc, gc_next, bx_ext, off_ext, vec, width):
    rows, total = gc.shape
    col = lambda h: (0, h)
    return pl.pallas_call(
        _conv_bwd_kernel,
        grid=(total // width,),
        in_specs=[
            pl.BlockSpec((rows, width), col),
            pl.BlockSpec((halo, width), col),
            pl.BlockSpec((rows + halo, width), col),
            pl.BlockSpec((rows + halo, 1), lambda h: (0, 0)),
            pl.BlockSpec((16, width), col),
        ],
        out_specs=[pl.BlockSpec((rows, width), col), pl.BlockSpec((8, width), col)],
        out_shape=[jax.ShapeDtypeStruct((rows, total), bf16), jax.ShapeDtypeStruct((8, total), f32)],
        scratch_shapes=[pltpu.VMEM((rows + halo, width), f32)],
        name="conv_bwd", cost_estimate=cost(7),
    )(gc, gc_next, bx_ext, off_ext, vec)


def after(x, *deps):
    return lax.optimization_barrier((x, deps))[0]


def per_device(
    tokens, cotangent, lengths, seq_deal, mixer_gain, recur_weight, gelu_weight, kernel_taps, kernel_bias,
    decay_param, rate_bias, input_bias, rate_blocks, input_blocks, mixer_out, feed_gain, feed_gate, feed_up,
    feed_down,
):
    groups = lax.axis_size("dp")
    lanes = lax.axis_size("tensor")
    bits = groups.bit_length() - 1
    g = lax.axis_index("dp")
    t = lax.axis_index("tensor")
    lane = t[None].astype(jnp.int32)
    device = g * lanes + t
    rows, width = tokens.shape
    piece_rows = rows // groups
    feats = mixer_gain.shape[0]
    chans = recur_weight.shape[1]
    lru_total = chans * lanes
    head_width = rate_blocks.shape[1]
    wide = tile_of(lru_total, 640)

    def swap(x, bit):
        return lax.ppermute(x, "dp", [(i, i ^ (1 << bit)) for i in range(groups)])

    def up(x):
        return lax.ppermute(x, "tensor", [(i, (i + 1) % lanes) for i in range(lanes)])

    def shift(x, by):
        return lax.ppermute(x, "tensor", [(i, i + by) for i in range(lanes) if 0 <= i + by < lanes])

    def gather_near(part, *deps):
        part = (after(part, *deps) if deps else part)[None]
        for bit in range(3, bits):
            part = jnp.concatenate([part, swap(part, bit)], axis=0)
        return part, swap(part, 1), swap(part, 2)

    def gather_far(near, *deps):
        part, from_x, from_y = near
        half = feats // 2
        low, high = after((from_y[..., :half, :], from_x[..., half:, :]), *deps)
        return part, from_x, from_y, swap(low, 1), swap(high, 2)

    def gather_outer(part, *deps):
        part = (after(part, *deps) if deps else part)[None]
        for bit in range(3, bits):
            part = jnp.concatenate([part, swap(part, bit)], axis=0)
        from_x, from_y = swap(part, 1), swap(part, 2)
        half = feats // 2
        low, high = swap(from_y[..., :half, :], 1), swap(from_x[..., half:, :], 2)
        return part, from_x, from_y, low, high

    def reduce_far(blocks):
        return swap(blocks[3], 1), swap(blocks[4], 2)

    def reduce_near(blocks, far):
        half = feats // 2
        to_x, to_y = blocks[1], blocks[2]
        y_low = to_y[..., :half, :].astype(f32) + far[0].astype(f32)
        to_y = jnp.concatenate([y_low.astype(bf16), to_y[..., half:, :]], axis=-2)
        x_high = to_x[..., half:, :].astype(f32) + far[1].astype(f32)
        to_x = jnp.concatenate([to_x[..., :half, :], x_high.astype(bf16)], axis=-2)
        return swap(to_x, 1), swap(to_y, 2)

    def reduce_end(blocks, near):
        total = blocks[0].astype(f32) + near[0].astype(f32) + near[1].astype(f32)
        for bit in reversed(range(3, bits)):
            keep = total.shape[0] // 2
            total = total[:keep] + swap(total[keep:].astype(bf16), bit).astype(f32)
        return total[0]

    feat_ids = jnp.arange(width, dtype=jnp.int32)
    block_ids, within = feat_ids // feats, feat_ids % feats
    rel_at = 2 * (block_ids % (groups // 2)) + block_ids // (groups // 2)
    from_in = (g ^ rel_at) * feats + within
    rel_of = g ^ block_ids
    from_out = ((rel_of & 1) * (groups // 2) + (rel_of >> 1)) * feats + within

    def vectors_out(x):
        lead = x.shape[0]
        y = jnp.moveaxis(x.reshape((lead,) + (2,) * bits + (feats,)), 1, bits)
        for bit in range(bits):
            y = jnp.where((g >> bit) & 1 == 1, jnp.flip(y, bits - bit), y)
        return y.reshape(lead, width)

    slots = jnp.arange(groups, dtype=jnp.int32)
    places = jnp.arange(seq_deal.shape[0], dtype=jnp.int32)
    own_ids = device * groups + slots
    place_of = jnp.sum(jnp.where(own_ids[:, None] == seq_deal[None, :], places[None, :], 0), axis=1)
    target = place_of // groups // lanes
    source = jnp.sum(jnp.where(own_ids[:, None] == places[None, :], seq_deal[None, :], 0), axis=1) // groups // lanes
    rel_group = slots ^ g
    send_order = jnp.sum(jnp.where(target[None, :] == rel_group[:, None], slots[None, :], 0), axis=1)
    back_order = jnp.sum(jnp.where(source[None, :] == rel_group[:, None], slots[None, :], 0), axis=1)

    def exchange(pieces, order):
        for bit in order:
            view = pieces.reshape((groups >> (bit + 1), 2, (1 << bit) * piece_rows, width))
            got = swap(view[:, 1], bit)
            pieces = jnp.stack([view[:, 0], got], axis=1)
        return pieces.reshape(groups, piece_rows, width)

    def deal(x, order):
        sent = pick_pieces(x.reshape(groups, piece_rows, width), send_order)
        return turn_feats(pick_pieces(exchange(sent, order), source ^ g).reshape(rows, width), from_in)

    def undeal(x, order):
        sent = pick_pieces(turn_feats(x, from_out).reshape(groups, piece_rows, width), back_order)
        return pick_pieces(exchange(sent, order), target ^ g).reshape(rows, width)

    x_first = [1, 2] + list(range(3, bits)) + [0]
    y_first = [2, 1] + list(range(3, bits)) + [0]

    row_place = t * rows + jnp.arange(rows + halo, dtype=jnp.int32)
    begins = jnp.zeros_like(row_place)
    start = jnp.int32(0)
    for s in range(lengths.shape[1]):
        begins = jnp.where(row_place >= start, start, begins)
        start = start + lengths[0, s]
    off_ext = jnp.where(row_place < lanes * rows, row_place - begins, -1)[:, None]

    chan_count = kernel_bias.shape[0]
    small = jnp.concatenate(
        [kernel_taps.reshape(-1), kernel_bias, rate_bias, input_bias, decay_param, mixer_gain, feed_gain]
    )
    small = jnp.pad(small, (0, -small.shape[0] % 128))[None, None]
    step = 1
    while step < lanes:
        got = lax.ppermute(small, "tensor", [(i, i ^ step) for i in range(lanes)])
        small = jnp.concatenate([small, got], axis=0)
        step *= 2
    small = small.reshape(1, lanes, -1)
    for bit in range(bits):
        small = jnp.concatenate([small, swap(small, bit)], axis=0)

    x_low = deal(tokens, x_first)
    x = x_low.astype(f32)
    cot_low = deal(cotangent, y_first)

    def over_lanes(w):
        return lax.all_gather(w, "tensor", axis=0)

    lanes_x = over_lanes(recur_weight)
    lanes_y = over_lanes(gelu_weight)
    blocks = jnp.stack([jnp.swapaxes(rate_blocks, 1, 2), jnp.swapaxes(input_blocks, 1, 2)])
    blocks = lax.all_gather(after(blocks, lanes_x), "dp", axis=2, tiled=True)
    rate_t, input_t = blocks[0], blocks[1]
    lanes_o = over_lanes(flip_weight(mixer_out))
    cot_all = lax.all_gather(after(cot_low, lanes_o), "tensor", axis=0, tiled=True)

    def with_other(own):
        return own, swap(own, 0)

    part_g = gather_outer(feed_gate)
    part_x = gather_outer(lanes_x)
    part_y = gather_outer(lanes_y, part_g[3:])
    wx = with_other(join_lanes(*part_x))
    part_o = gather_outer(lanes_o, part_x[3:], cot_low)
    wg = with_other(join_feats(*part_g))
    wy = with_other(join_lanes(*part_y))
    wo = with_other(join_lanes(*part_o))

    chan_ids = jnp.arange(lru_total, dtype=jnp.int32)
    chan_lane, chan_dp, chan_in = chan_ids // chans, chan_ids % chans // chan_count, chan_ids % chan_count
    from_chan = ((chan_dp ^ g) * lanes + (chan_lane ^ t)) * chan_count + chan_in
    from_gain = (g ^ rel_at ^ g) * feats + within
    small_cols = 8 * chan_count
    chan_part = small[:, :, :small_cols].reshape(groups, lanes, 8, chan_count)
    chan_part = jnp.moveaxis(chan_part, 2, 0).reshape(8, lru_total)
    gain_part = small[:, 0, small_cols : small_cols + 2 * feats].reshape(groups, 2, feats)
    gain_part = jnp.swapaxes(gain_part, 0, 1).reshape(2, width)
    chan_vec = turn_feats(jnp.pad(chan_part, ((0, 8), (0, 0))), from_chan).astype(f32)
    gains = turn_feats(jnp.pad(gain_part, ((0, 14), (0, 0))), from_gain).astype(f32)
    gain_first, gain_second = gains[0], gains[1]
    vec = jnp.concatenate(
        [
            chan_vec[:7],
            jax.nn.softplus(-chan_vec[7:8]),
            jax.nn.sigmoid(-chan_vec[7:8]),
            jnp.zeros((7, lru_total), f32),
        ],
        axis=0,
    )

    normed_low = (x * inv_rms(x) * gain_first[None]).astype(bf16)
    normed_ext = jnp.concatenate([up(normed_low[rows - halo :]), normed_low], axis=0)
    bx_ext = rows_into(normed_ext, wx)
    near_u = gather_near(feed_up, part_y[3:], bx_ext)
    by = rows_into(normed_low, wy)
    conv_low, state_loc, prod_loc = mix_fwd(bx_ext, off_ext, vec, rate_t, input_t)
    near_d = gather_near(flip_weight(feed_down), part_o[3:], state_loc)
    edge = jnp.concatenate([state_loc[rows - 1 :], prod_loc[rows - 1 :], jnp.zeros((6, lru_total), f32)], axis=0)

    def carry_in(edge, direction):
        total = jnp.zeros((1, lru_total), f32)
        factor = jnp.ones((1, lru_total), f32)
        for by_lanes in range(1, lanes):
            far = shift(edge, direction * by_lanes)
            total = total + factor * far[0:1]
            factor = factor * far[1:2]
        return jnp.broadcast_to(total, (8, lru_total))

    enter = carry_in(edge, 1)
    state, mixed = mix_out(state_loc, prod_loc, enter, by, wide)
    middle = x + rows_back([(mixed, wo)])
    ns_low = (middle * inv_rms(middle) * gain_second[None]).astype(bf16)
    part_u = gather_far(near_u, ns_low)
    part_d = gather_far(near_d, ns_low)
    ns_rows = [ns_low]
    for _ in range(lanes - 1):
        ns_rows.append(up(ns_rows[-1]))

    part_u = (after(part_u[0], ns_rows[1]),) + tuple(part_u[1:])
    part_d = (after(part_d[0], ns_rows[1]),) + tuple(part_d[1:])
    wu = with_other(join_feats(*part_u))
    wd = with_other(join_feats(*part_d))

    pair = 2
    hidden, g_gate, g_up = [], [], []
    total = None
    for at in range(0, lanes, pair):
        first = ns_rows[at] if total is None else after(ns_rows[at], total)
        h, gg, gu = feed_pair([first] + ns_rows[at + 1 : at + pair], cot_all, at, wg, wu, wd, lane, lanes)
        hidden.append(h)
        g_gate.append(gg)
        g_up.append(gu)
        if total is None:
            total = feed_back([(gg, wg), (gu, wu)], 1, rows, [], bf16)

    def other_half(lefts, rights, *deps, **kind):
        first = after(rights[0], *deps) if deps else rights[0]
        return weight_grad(lefts, [first] + rights[1:], 1, feats, lane, lanes, **kind)

    def own_half(lefts, rights, other, *deps, **kind):
        first = after(rights[0], *deps) if deps else rights[0]
        return weight_grad(lefts, [first] + rights[1:], 0, feats, lane, lanes, got=swap(other, 0), **kind)

    def second_part(k, total, *deps):
        terms = [(after(g_gate[k // pair], *deps) if deps else g_gate[k // pair], wg), (g_up[k // pair], wu)]
        return feed_back(terms, k % pair, rows, [] if total is None else [up(total)], f32 if k == 0 else bf16)

    cot_parts = [(cot_all, rows, k) for k in range(lanes)]
    for k in range(2, lanes - 2):
        total = second_part(k, total)
    total = second_part(lanes - 2, total)
    other_down = other_half(cot_parts, hidden, total)
    other_gate = other_half(ns_rows, g_gate, other_down)
    own_down = own_half(cot_parts, hidden, other_down, other_gate)
    far_down = reduce_far(own_down)
    own_gate = own_half(ns_rows, g_gate, other_gate, own_down)
    far_gate = reduce_far(own_gate)
    total = second_part(lanes - 1, total, own_gate, far_down)
    near_down = reduce_near(own_down, far_down)
    other_up = other_half(ns_rows, g_up, total)
    near_gate = reduce_near(own_gate, far_gate)
    own_up = own_half(ns_rows, g_up, other_up, far_gate)
    far_up = reduce_far([after(b, near_down) for b in own_up])
    g_second = second_part(0, total, own_up, near_down)
    near_up = reduce_near(own_up, far_up)

    g_mid_part, d_gain_second = norm_back(middle, gain_second[None], g_second)
    g_middle = cot_low.astype(f32) + g_mid_part
    g1 = g_middle.astype(bf16)

    def lane_sum(blocks):
        return lax.psum_scatter(blocks.astype(bf16), "tensor", scatter_dimension=0).astype(f32)

    by_lane = dict(by_lane=True)
    other_out = other_half([g1], [mixed], **by_lane)
    gm = rows_into(after(g1, other_out, near_gate), wo)
    own_out = own_half([g1], [mixed], other_out, gm, far_up, **by_lane)
    far_out = reduce_far(own_out)
    gy_low, adj_loc, tail, edge_back = mix_adj(after(gm, own_out), by, state, conv_low, off_ext, vec, rate_t)
    hand = carry_in(edge_back, -1)
    other_y = other_half([normed_low], [gy_low], near_up, **by_lane)
    near_out = reduce_near(own_out, far_out)
    feed_sum = feed_out([after(hidden[0], other_y, far_out)] + hidden[1:], wd, lane, lanes)
    feed_sum = lax.psum_scatter(feed_sum, "tensor", scatter_dimension=0, tiled=True)
    own_y = own_half([normed_low], [gy_low], other_y, **by_lane)
    far_y = reduce_far(own_y)
    g_conv, d_rate, d_input, sums_gate = mix_bwd(
        after(adj_loc, own_y), tail, hand, state, enter, conv_low, off_ext, vec, rate_t, input_t
    )
    gc_next = lax.ppermute(g_conv[:halo], "tensor", [(i, (i - 1) % lanes) for i in range(lanes)])
    gx_low, sums_conv = conv_bwd(g_conv, gc_next, bx_ext, off_ext, vec, wide)
    near_y = reduce_near(own_y, far_y)
    other_x = other_half([normed_low], [gx_low], near_out, **by_lane)
    g_first = rows_back([(after(gx_low, other_x), wx), (gy_low, wy)])
    own_x = own_half([normed_low], [gx_low], other_x, far_y, **by_lane)
    far_x = reduce_far(own_x)
    d_down = reduce_end(own_down, near_down)
    d_gate = reduce_end(own_gate, near_gate)
    d_up = reduce_end(own_up, near_up)
    d_out = lane_sum(reduce_end(own_out, near_out))
    near_x = reduce_near(own_x, far_x)
    d_y = lane_sum(reduce_end(own_y, near_y))
    d_x = lane_sum(reduce_end(own_x, near_x))
    g_tok_part, d_gain_first = norm_back(x, gain_first[None], g_first)
    tokens_grad = undeal((g_middle + g_tok_part).astype(bf16), y_first)
    block_out = undeal((middle + feed_sum.astype(f32)).astype(bf16), x_first)

    d_blocks = lax.psum_scatter(jnp.stack([d_rate, d_input]), "dp", scatter_dimension=2, tiled=True)
    d_blocks = jnp.swapaxes(lax.psum(d_blocks, "tensor"), 2, 3).astype(f32)
    d_gains = vectors_out(jnp.stack([d_gain_first, d_gain_second]))
    vectors = jnp.concatenate([sums_conv[:5], sums_gate[:3], d_gains, jnp.zeros((6, width), f32)], axis=0)
    for bit in range(bits):
        vectors = vectors + swap(vectors, bit)
    step = 1
    while step < lanes:
        vectors = vectors + lax.ppermute(vectors, "tensor", [(i, i ^ step) for i in range(lanes)])
        step *= 2
    chan_grad = lax.dynamic_slice_in_dim(vectors[:8], (t * groups + g) * chan_count, chan_count, axis=1)
    gain_grad = lax.dynamic_slice_in_dim(vectors[8:10], g * feats, feats, axis=1)

    return (
        block_out,
        tokens_grad,
        gain_grad[0],
        d_x,
        d_y,
        chan_grad[0:4],
        chan_grad[4],
        chan_grad[5],
        chan_grad[6],
        chan_grad[7],
        d_blocks[0],
        d_blocks[1],
        d_out.T,
        gain_grad[1],
        d_gate,
        d_up,
        d_down.T,
    )


def solution(mesh):
    rows = P(("dp", "tensor"), None)
    feat = P("dp")
    chan = P(("tensor", "dp"))
    taps = P(None, ("tensor", "dp"))
    into = P("dp", "tensor")
    back = P("tensor", "dp")
    blocks = P(None, None, "dp")
    in_specs = (
        rows, rows, P("dp", None), P(), feat, into, into, taps, chan, chan, chan, chan, blocks, blocks, back, feat,
        into, into, back,
    )
    out_specs = (
        rows, rows, feat, into, into, taps, chan, chan, chan, chan, blocks, blocks, back, feat, into, into, back,
    )
    return jax.shard_map(per_device, mesh=mesh, in_specs=in_specs, out_specs=out_specs, check_vma=False)
```

```python
import functools

import jax
import jax.numpy as jnp
from jax import lax
from jax.experimental import pallas as pl
from jax.experimental.pallas import tpu as pltpu
from jax.sharding import PartitionSpec as P

norm_eps = 1e-06
scale_floor = 0.001
halo = 8
bf16 = jnp.bfloat16
f32 = jnp.float32
gelu_c = 0.7978845608028654
gelu_k = 0.044715


def gelu_both(x):
    sq = x * x
    th = jnp.tanh(gelu_c * x * (1.0 + gelu_k * sq))
    half = 0.5 * (1.0 + th)
    return x * half, half + 0.5 * x * (1.0 - th * th) * gelu_c * (1.0 + 3.0 * gelu_k * sq)


def inv_rms(x):
    return lax.rsqrt(jnp.mean(x * x, axis=-1, keepdims=True) + norm_eps)


def norm_back(x, gain, grad):
    r = inv_rms(x)
    v = gain * grad
    dx = r * v - x * (r * r * r) * jnp.mean(x * v, axis=-1, keepdims=True)
    return dx, jnp.sum(grad * x * r, axis=0)


def mm(a, b):
    return jnp.dot(a, b, preferred_element_type=f32)


def mm_nt(a, b):
    return lax.dot_general(a, b, (((1,), (1,)), ((), ())), preferred_element_type=f32)


def mm_tn(a, b):
    return lax.dot_general(a, b, (((0,), (0,)), ((), ())), preferred_element_type=f32)


roomy = pltpu.CompilerParams(vmem_limit_bytes=56 * 1024 * 1024)


def cost(microseconds):
    return pl.CostEstimate(flops=int(microseconds * 1.15e9), bytes_accessed=1024, transcendentals=0)


def tile_of(total, most):
    for tile in range(most - most % 128, 0, -128):
        if total % tile == 0:
            return tile
    return total


def _pick_kernel(order_ref, x_ref, o_ref):
    for i in range(o_ref.shape[0]):
        o_ref[i] = x_ref[order_ref[i]]


def pick_pieces(pieces, order):
    return pl.pallas_call(
        _pick_kernel,
        in_specs=[pl.BlockSpec(memory_space=pltpu.SMEM), pl.BlockSpec(memory_space=pltpu.VMEM)],
        out_specs=pl.BlockSpec(memory_space=pltpu.VMEM),
        out_shape=jax.ShapeDtypeStruct(pieces.shape, pieces.dtype),
        name="pick_pieces", cost_estimate=cost(2),
    )(order, pieces)


def _turn_kernel(from_ref, x_ref, o_ref):
    width = x_ref.shape[1]
    place = lax.broadcasted_iota(jnp.int32, (width, o_ref.shape[1]), 0)
    hot = jnp.where(place == from_ref[...], 1.0, 0.0).astype(bf16)
    o_ref[...] = mm(x_ref[...], hot).astype(bf16)


def turn_feats(x, from_feat):
    rows, width = x.shape
    tile = tile_of(width, 512)
    return pl.pallas_call(
        _turn_kernel,
        grid=(width // tile,),
        in_specs=[pl.BlockSpec((1, tile), lambda j: (0, j)), pl.BlockSpec((rows, width), lambda j: (0, 0))],
        out_specs=pl.BlockSpec((rows, tile), lambda j: (0, j)),
        out_shape=jax.ShapeDtypeStruct(x.shape, bf16),
        compiler_params=roomy,
        name="turn_feats", cost_estimate=cost(6),
    )(from_feat[None], x)


def unit(n):
    one = lax.broadcasted_iota(jnp.int32, (n, n), 0) == lax.broadcasted_iota(jnp.int32, (n, n), 1)
    return jnp.where(one, 1.0, 0.0).astype(bf16)


def _flip_kernel(x_ref, o_ref):
    o_ref[...] = mm_tn(x_ref[...], unit(x_ref.shape[0])).astype(bf16)


def flip_weight(x):
    rows, cols = x.shape
    tile = tile_of(rows, 640)
    return pl.pallas_call(
        _flip_kernel,
        grid=(rows // tile,),
        in_specs=[pl.BlockSpec((tile, cols), lambda j: (j, 0))],
        out_specs=pl.BlockSpec((cols, tile), lambda j: (0, j)),
        out_shape=jax.ShapeDtypeStruct((cols, rows), bf16),
        compiler_params=roomy,
        name="flip_weight", cost_estimate=cost(4),
    )(x)


def _join_kernel(own_ref, x_ref, y_ref, low_ref, high_ref, out_ref):
    extra, feats = own_ref.shape[0], own_ref.shape[1]
    half = feats // 2
    for e in range(extra):
        for q, ref in enumerate((own_ref, x_ref, y_ref)):
            out_ref[(4 * e + q) * feats : (4 * e + q + 1) * feats] = ref[e]
        at = (4 * e + 3) * feats
        out_ref[at : at + half] = low_ref[e]
        out_ref[at + half : at + feats] = high_ref[e]


def join_feats(own, from_x, from_y, low, high):
    extra, feats, cols = own.shape
    tile = tile_of(cols, 640)
    full = pl.BlockSpec((extra, feats, tile), lambda j: (0, 0, j))
    part = pl.BlockSpec((extra, feats // 2, tile), lambda j: (0, 0, j))
    rows = extra * 4 * feats
    return pl.pallas_call(
        _join_kernel,
        grid=(cols // tile,),
        in_specs=[full, full, full, part, part],
        out_specs=pl.BlockSpec((rows, tile), lambda j: (0, j)),
        out_shape=jax.ShapeDtypeStruct((rows, cols), bf16),
        compiler_params=roomy,
        name="join_feats", cost_estimate=cost(5.5),
    )(own, from_x, from_y, low, high)


def _join_lanes_kernel(own_ref, x_ref, y_ref, low_ref, high_ref, out_ref):
    extra, feats = own_ref.shape[0], own_ref.shape[2]
    half = feats // 2
    for e in range(extra):
        for q, ref in enumerate((own_ref, x_ref, y_ref)):
            out_ref[0, (4 * e + q) * feats : (4 * e + q + 1) * feats] = ref[e, 0]
        at = (4 * e + 3) * feats
        out_ref[0, at : at + half] = low_ref[e, 0]
        out_ref[0, at + half : at + feats] = high_ref[e, 0]


def join_lanes(own, from_x, from_y, low, high):
    extra, lanes, feats, chans = own.shape
    full = pl.BlockSpec((extra, 1, feats, chans), lambda k: (0, k, 0, 0))
    part = pl.BlockSpec((extra, 1, feats // 2, chans), lambda k: (0, k, 0, 0))
    rows = extra * 4 * feats
    return pl.pallas_call(
        _join_lanes_kernel,
        grid=(lanes,),
        in_specs=[full, full, full, part, part],
        out_specs=pl.BlockSpec((1, rows, chans), lambda k: (k, 0, 0)),
        out_shape=jax.ShapeDtypeStruct((lanes, rows, chans), bf16),
        compiler_params=roomy,
        name="join_lanes",
        cost_estimate=cost(5),
    )(own, from_x, from_y, low, high)


def chan_spec(rows, chans):
    if chans % 128 == 0:
        return pl.BlockSpec((rows, chans), lambda k: (0, k))
    return pl.BlockSpec((1, rows, chans), lambda k: (k, 0, 0))


def chan_in(x, chans):
    if chans % 128 == 0:
        return x
    return jnp.swapaxes(x.reshape(x.shape[0], -1, chans), 0, 1)


def chan_get(ref):
    return ref[...] if len(ref.shape) == 2 else ref[0]


def rows_into(a, weight):
    rows, width = a.shape
    lanes, half, chans = weight[0].shape
    flat = chans % 128 == 0

    def kernel(a_ref, own_ref, other_ref, out_ref):
        got = mm(a_ref[:, :half], own_ref[0]) + mm(a_ref[:, half:], other_ref[0])
        if flat:
            out_ref[...] = got
        else:
            out_ref[0] = got

    block = pl.BlockSpec((1, half, chans), lambda k: (k, 0, 0))
    out = pl.pallas_call(
        kernel,
        grid=(lanes,),
        in_specs=[pl.BlockSpec((rows, width), lambda k: (0, 0)), block, block],
        out_specs=chan_spec(rows, chans),
        out_shape=jax.ShapeDtypeStruct((rows, lanes * chans) if flat else (lanes, rows, chans), f32),
        compiler_params=roomy,
        name="rows_into",
        cost_estimate=cost(11),
    )(a, *weight)
    return out if flat else jnp.swapaxes(out, 0, 1).reshape(rows, lanes * chans)


def rows_back(terms):
    rows = terms[0][0].shape[0]
    lanes, half, chans = terms[0][1][0].shape
    pairs = len(terms)

    def kernel(*refs):
        out_ref = refs[-1]

        @pl.when(pl.program_id(0) == 0)
        def _():
            out_ref[...] = jnp.zeros_like(out_ref)

        for side in range(2):
            total = None
            for p in range(pairs):
                part = mm_nt(chan_get(refs[p]), refs[pairs + 2 * p + side][0])
                total = part if total is None else total + part
            cols = slice(side * half, (side + 1) * half)
            out_ref[:, cols] = out_ref[:, cols] + total

    block = pl.BlockSpec((1, half, chans), lambda k: (k, 0, 0))
    arrays = [chan_in(b, chans) for b, _ in terms]
    for _, weight in terms:
        arrays += list(weight)
    return pl.pallas_call(
        kernel,
        grid=(lanes,),
        in_specs=[chan_spec(rows, chans)] * pairs + [block] * (2 * pairs),
        out_specs=pl.BlockSpec((rows, 2 * half), lambda k: (0, 0)),
        out_shape=jax.ShapeDtypeStruct((rows, 2 * half), f32),
        compiler_params=roomy,
        name="rows_back",
        cost_estimate=cost(8 * pairs + 3),
    )(*arrays)


def lane_block(lane, k, lanes):
    return lax.rem(lane[0] - k + lanes, lanes)


def feed_pair(ns, cot_all, at, gate, up, down, lane, lanes):
    count = len(ns)
    rows, width = ns[0].shape
    half, hidden = gate[0].shape
    tile = tile_of(hidden, 640)

    def kernel(lane_ref, *refs):
        ns_refs, cot_refs = refs[:count], refs[count : 2 * count]
        weights = refs[2 * count : 2 * count + 6]
        hid_ref, gate_ref, up_ref, ns_all, cot_rows = refs[2 * count + 6 :]

        @pl.when(pl.program_id(0) == 0)
        def _():
            for i in range(count):
                ns_all[i * rows : (i + 1) * rows] = ns_refs[i][...]
                cot_rows[i * rows : (i + 1) * rows] = cot_refs[i][...]

        def times(a, i):
            return mm(a[:, :half], weights[i][...]) + mm(a[:, half:], weights[i + 1][...])

        act, slope = gelu_both(times(ns_all, 0))
        up_pre = times(ns_all, 2)
        hid_ref[...] = (act * up_pre).astype(bf16)
        grad = times(cot_rows, 4)
        gate_ref[...] = (grad * up_pre * slope).astype(bf16)
        up_ref[...] = (grad * act).astype(bf16)

    whole = pl.BlockSpec((rows, width), lambda j, lane: (0, 0))
    cots = [
        pl.BlockSpec((rows, width), functools.partial(lambda j, lane, k: (lane_block(lane, k, lanes), 0), k=at + i))
        for i in range(count)
    ]
    piece = pl.BlockSpec((half, tile), lambda j, lane: (0, j))
    out = pl.BlockSpec((count * rows, tile), lambda j, lane: (0, j))
    return pl.pallas_call(
        kernel,
        grid_spec=pltpu.PrefetchScalarGridSpec(
            num_scalar_prefetch=1,
            grid=(hidden // tile,),
            in_specs=[whole] * count + cots + [piece] * 6,
            out_specs=[out] * 3,
            scratch_shapes=[pltpu.VMEM((count * rows, width), bf16)] * 2,
        ),
        out_shape=[jax.ShapeDtypeStruct((count * rows, hidden), bf16)] * 3,
        compiler_params=roomy,
        name="feed_pair",
        cost_estimate=cost(27),
    )(lane, *ns, *([cot_all] * count), *gate, *up, *down)


def feed_back(terms, at, rows, adds, kind):
    half, hidden = terms[0][1][0].shape
    width = 2 * half
    tile = tile_of(half, 640)
    steps = half // tile
    pairs = len(terms)

    def kernel(*refs):
        out_ref = refs[-1]
        j = pl.program_id(0)
        for side in range(2):

            @pl.when((j < steps) if side == 0 else (j >= steps))
            def _():
                total = None
                for p in range(pairs):
                    part = mm_nt(refs[p][...], refs[pairs + 2 * p + side][...])
                    total = part if total is None else total + part
                for extra_ref in refs[3 * pairs : -1]:
                    total = total + extra_ref[...].astype(f32)
                out_ref[...] = total.astype(kind)

    specs = [pl.BlockSpec((rows, hidden), lambda j: (at, 0))] * pairs
    arrays = [b for b, _ in terms]
    for _, weight in terms:
        specs.append(pl.BlockSpec((tile, hidden), lambda j: (jnp.minimum(j, steps - 1), 0)))
        specs.append(pl.BlockSpec((tile, hidden), lambda j: (jnp.maximum(j - steps, 0), 0)))
        arrays += list(weight)
    specs += [pl.BlockSpec((rows, tile), lambda j: (0, j))] * len(adds)
    return pl.pallas_call(
        kernel,
        grid=(2 * steps,),
        in_specs=specs,
        out_specs=pl.BlockSpec((rows, tile), lambda j: (0, j)),
        out_shape=jax.ShapeDtypeStruct((rows, width), kind),
        compiler_params=roomy,
        name="feed_back",
        cost_estimate=cost(13),
    )(*arrays, *adds)


def feed_out(hidden, weight, lane, lanes):
    half, units = weight[0].shape
    width = 2 * half
    tile = tile_of(half, 640)
    steps = half // tile
    many = len(hidden)
    count = lanes // many
    rows = hidden[0].shape[0] // count

    def kernel(lane_ref, *refs):
        out_ref = refs[-1]
        j = pl.program_id(0)
        for side in range(2):

            @pl.when((j < steps) if side == 0 else (j >= steps))
            def _():
                for i in range(many):
                    got = mm_nt(refs[i][...], refs[many + side][...]).astype(bf16)
                    for c in range(count):
                        at = lane_block(lane_ref, i * count + c, lanes) * rows
                        out_ref[pl.ds(pl.multiple_of(at, rows), rows)] = got[c * rows : (c + 1) * rows]

    whole = pl.BlockSpec((count * rows, units), lambda j, lane: (0, 0))
    return pl.pallas_call(
        kernel,
        grid_spec=pltpu.PrefetchScalarGridSpec(
            num_scalar_prefetch=1,
            grid=(2 * steps,),
            in_specs=[whole] * many
            + [
                pl.BlockSpec((tile, units), lambda j, lane: (jnp.minimum(j, steps - 1), 0)),
                pl.BlockSpec((tile, units), lambda j, lane: (jnp.maximum(j - steps, 0), 0)),
            ],
            out_specs=pl.BlockSpec((lanes * rows, tile), lambda j, lane: (0, j)),
        ),
        out_shape=jax.ShapeDtypeStruct((lanes * rows, width), bf16),
        compiler_params=roomy,
        name="feed_out",
        cost_estimate=cost(18),
    )(lane, *hidden, *weight)


def weight_grad(lefts, rights, side, feats, lane, lanes, got=None, by_lane=False):
    specs, arrays = [], []
    for left in lefts:
        if isinstance(left, tuple):
            array, left_rows, k = left
            pick = functools.partial(lambda j, lane, k: (lane_block(lane, k, lanes), side), k=k)
        else:
            array, left_rows, pick = left, left.shape[0], lambda j, lane: (0, side)
        half = array.shape[1] // 2
        specs.append(pl.BlockSpec((left_rows, half), pick))
        arrays.append(array)
    count = len(lefts)
    right_rows, cols = rights[0].shape
    many = len(rights)
    tile = cols // lanes if by_lane else tile_of(cols, 640)
    extra = half // (4 * feats)
    part = feats // 2

    def kernel(lane_ref, *refs):
        left_refs, right_refs = refs[:count], refs[count : count + many]
        rest = refs[count + many :]
        if count > 1:
            all_ref, rest = rest[-1], rest[:-1]

            @pl.when(pl.program_id(0) == 0)
            def _():
                for i in range(count):
                    all_ref[i * left_rows : (i + 1) * left_rows] = left_refs[i][...]
        else:
            all_ref = left_refs[0]
        total = None
        for i in range(many):
            piece = mm_tn(all_ref[i * right_rows : (i + 1) * right_rows], chan_get(right_refs[i]))
            total = piece if total is None else total + piece
        if got is None:
            if by_lane:
                rest[0][0] = total.astype(bf16)
            else:
                rest[0][...] = total.astype(bf16)
            return
        total = (total + chan_get(rest[0]).astype(f32)).astype(bf16)
        cuts = (0, feats, 2 * feats, 3 * feats, 3 * feats + part, 4 * feats)
        for e in range(extra):
            base = 4 * feats * e
            for ref, a, b in zip(rest[1:], cuts[:-1], cuts[1:]):
                if by_lane:
                    ref[e, 0] = total[base + a : base + b]
                else:
                    ref[e] = total[base + a : base + b]

    flat = not by_lane or tile % 128 == 0
    if flat:
        right_spec = pl.BlockSpec((right_rows, tile), lambda j, lane: (0, j))
    else:
        right_spec = pl.BlockSpec((1, right_rows, tile), lambda j, lane: (j, 0, 0))
        rights = [chan_in(r, tile) for r in rights]
    if by_lane:
        sent, sent_shape = pl.BlockSpec((1, half, tile), lambda j, lane: (j, 0, 0)), (lanes, half, tile)
        block = lambda n: pl.BlockSpec((extra, 1, n, tile), lambda j, lane: (0, j, 0, 0))
        block_shape = lambda n: (extra, lanes, n, tile)
    else:
        sent, sent_shape = pl.BlockSpec((half, tile), lambda j, lane: (0, j)), (half, cols)
        block = lambda n: pl.BlockSpec((extra, n, tile), lambda j, lane: (0, 0, j))
        block_shape = lambda n: (extra, n, cols)
    sizes = (feats, feats, feats, part, part)
    specs += [right_spec] * many
    arrays += list(rights)
    if got is None:
        out_specs, out_shape = sent, jax.ShapeDtypeStruct(sent_shape, bf16)
    else:
        specs.append(sent)
        arrays.append(got)
        out_specs = [block(n) for n in sizes]
        out_shape = [jax.ShapeDtypeStruct(block_shape(n), bf16) for n in sizes]
    return pl.pallas_call(
        kernel,
        grid_spec=pltpu.PrefetchScalarGridSpec(
            num_scalar_prefetch=1,
            grid=(cols // tile,),
            in_specs=specs,
            out_specs=out_specs,
            scratch_shapes=[pltpu.VMEM((left_rows * count, half), bf16)] if count > 1 else [],
        ),
        out_shape=out_shape,
        compiler_params=roomy,
        name="weight_grad",
        cost_estimate=cost(10 if count > 1 else 7),
    )(lane, *arrays)


def scan_rows(a, b, reverse):
    rows = a.shape[0]
    place = lax.broadcasted_iota(jnp.int32, a.shape, 0)
    step = 1
    while step < rows:
        if reverse:
            inside = place < rows - step
            turn = rows - step
        else:
            inside = place >= step
            turn = step
        a_far = jnp.where(inside, pltpu.roll(a, turn, 0), 1.0)
        b_far = jnp.where(inside, pltpu.roll(b, turn, 0), 0.0)
        b = a * b_far + b
        a = a * a_far
        step *= 2
    return a, b


def gate_values(conv_low, rate_t, input_t, vec, first):
    q = jax.nn.sigmoid(mm_nt(conv_low, rate_t) + vec[5:6])
    p = jax.nn.sigmoid(mm_nt(conv_low, input_t) + vec[6:7])
    decay = jnp.where(first, 0.0, jnp.exp(-8.0 * q * vec[7:8]))
    room = 1.0 - decay * decay
    scale = jnp.sqrt(jnp.maximum(room, scale_floor))
    return q, p, decay, room, scale


def _mix_fwd_kernel(bx_ref, off_ref, vec_ref, rate_ref, input_ref, conv_ref, state_ref, prod_ref):
    rows = conv_ref.shape[0]
    off = off_ref[0:rows]
    vec = vec_ref[...]
    conv = jnp.broadcast_to(vec[4:5], state_ref.shape)
    for lag in range(4):
        conv = conv + jnp.where(off >= lag, bx_ref[halo - lag : halo - lag + rows], 0.0) * vec[lag : lag + 1]
    conv_low = conv.astype(bf16)
    conv_ref[...] = conv_low
    q, p, decay, room, scale = gate_values(conv_low, rate_ref[0], input_ref[0], vec, off == 0)
    driven = scale * p * conv_low.astype(f32)
    prod, state = scan_rows(decay, driven, False)
    state_ref[...] = state
    prod_ref[...] = prod


def mix_fwd(bx_ext, off_ext, vec, rate_t, input_t):
    heads, width, _ = rate_t.shape
    ext = bx_ext.shape[0]
    rows = ext - halo
    col = lambda h: (0, h)
    return pl.pallas_call(
        _mix_fwd_kernel,
        grid=(heads,),
        in_specs=[
            pl.BlockSpec((ext, width), col),
            pl.BlockSpec((ext, 1), lambda h: (0, 0)),
            pl.BlockSpec((16, width), col),
            pl.BlockSpec((1, width, width), lambda h: (h, 0, 0)),
            pl.BlockSpec((1, width, width), lambda h: (h, 0, 0)),
        ],
        out_specs=[pl.BlockSpec((rows, width), col)] * 3,
        out_shape=[
            jax.ShapeDtypeStruct((rows, heads * width), bf16),
            jax.ShapeDtypeStruct((rows, heads * width), f32),
            jax.ShapeDtypeStruct((rows, heads * width), f32),
        ],
        name="mix_fwd", cost_estimate=cost(12),
    )(bx_ext, off_ext, vec, rate_t, input_t)


def _mix_out_kernel(state_ref, prod_ref, enter_ref, by_ref, full_ref, mixed_ref):
    state = state_ref[...] + prod_ref[...] * enter_ref[0:1]
    full_ref[...] = state
    act, _ = gelu_both(by_ref[...])
    mixed_ref[...] = (state * act).astype(bf16)


def mix_out(state, prod, enter, by, width):
    rows, total = state.shape
    blk = pl.BlockSpec((rows, width), lambda h: (0, h))
    return pl.pallas_call(
        _mix_out_kernel,
        grid=(total // width,),
        in_specs=[blk, blk, pl.BlockSpec((8, width), lambda h: (0, h)), blk],
        out_specs=[blk, blk],
        out_shape=[jax.ShapeDtypeStruct((rows, total), f32), jax.ShapeDtypeStruct((rows, total), bf16)],
        name="mix_out", cost_estimate=cost(6),
    )(state, prod, enter, by)


def _mix_adj_kernel(gm_ref, by_ref, full_ref, conv_ref, off_ref, vec_ref, rate_ref, gy_ref, adj_ref, tail_ref, edge_ref):
    rows = conv_ref.shape[0]
    vec = vec_ref[...]
    off = off_ref[0:rows]
    q = jax.nn.sigmoid(mm_nt(conv_ref[...], rate_ref[0]) + vec[5:6])
    decay = jnp.where(off == 0, 0.0, jnp.exp(-8.0 * q * vec[7:8]))
    act, act_grad = gelu_both(by_ref[...])
    gm = gm_ref[...]
    gy_ref[...] = (gm * full_ref[...] * act_grad).astype(bf16)
    place = lax.broadcasted_iota(jnp.int32, decay.shape, 0)
    after = jnp.where(place == rows - 1, 1.0, pltpu.roll(decay, rows - 1, 0))
    tail, adj = scan_rows(after, gm * act, True)
    adj_ref[...] = adj
    tail_ref[...] = tail
    edge_ref[0:1] = decay[0:1] * adj[0:1]
    edge_ref[1:2] = decay[0:1] * tail[0:1]
    edge_ref[2:8] = jnp.zeros((6, decay.shape[1]), f32)


def mix_adj(gm, by, full, conv, off_ext, vec, rate_t):
    heads, width, _ = rate_t.shape
    rows, total = gm.shape
    blk = pl.BlockSpec((rows, width), lambda h: (0, h))
    return pl.pallas_call(
        _mix_adj_kernel,
        grid=(heads,),
        in_specs=[
            blk,
            blk,
            blk,
            blk,
            pl.BlockSpec((rows + halo, 1), lambda h: (0, 0)),
            pl.BlockSpec((16, width), lambda h: (0, h)),
            pl.BlockSpec((1, width, width), lambda h: (h, 0, 0)),
        ],
        out_specs=[blk, blk, blk, pl.BlockSpec((8, width), lambda h: (0, h))],
        out_shape=[
            jax.ShapeDtypeStruct((rows, total), bf16),
            jax.ShapeDtypeStruct((rows, total), f32),
            jax.ShapeDtypeStruct((rows, total), f32),
            jax.ShapeDtypeStruct((8, total), f32),
        ],
        name="mix_adj", cost_estimate=cost(13),
    )(gm, by, full, conv, off_ext, vec, rate_t)


def _mix_bwd_kernel(
    adj_ref, tail_ref, hand_ref, full_ref, enter_ref, conv_ref, off_ref, vec_ref, rate_ref, input_ref,
    gc_ref, drate_ref, dinput_ref, sums_ref,
):
    rows = conv_ref.shape[0]
    vec = vec_ref[...]
    off = off_ref[0:rows]
    conv_low = conv_ref[...]
    conv = conv_low.astype(f32)
    rate_t, input_t = rate_ref[0], input_ref[0]
    q, p, decay, room, scale = gate_values(conv_low, rate_t, input_t, vec, off == 0)
    adj = adj_ref[...] + tail_ref[...] * hand_ref[0:1]
    place = lax.broadcasted_iota(jnp.int32, adj.shape, 0)
    before = jnp.where(place == 0, enter_ref[0:1], pltpu.roll(full_ref[...], 1, 0))
    g_decay = adj * before - jnp.where(room > scale_floor, adj * p * conv * decay / scale, 0.0)
    g_log = g_decay * decay
    g_rate = (-8.0 * g_log * vec[7:8] * q * (1.0 - q)).astype(bf16)
    g_input = (adj * scale * conv * p * (1.0 - p)).astype(bf16)
    gc_ref[...] = adj * scale * p + mm(g_rate, rate_t) + mm(g_input, input_t)
    drate_ref[0] = mm_tn(g_rate, conv_low).astype(bf16)
    dinput_ref[0] = mm_tn(g_input, conv_low).astype(bf16)
    sums_ref[0:1] = jnp.sum(8.0 * g_log * q, axis=0, keepdims=True) * vec[8:9]
    sums_ref[1:2] = jnp.sum(g_rate.astype(f32), axis=0, keepdims=True)
    sums_ref[2:3] = jnp.sum(g_input.astype(f32), axis=0, keepdims=True)
    sums_ref[3:8] = jnp.zeros((5, adj.shape[1]), f32)


def mix_bwd(adj, tail, hand, full, enter, conv, off_ext, vec, rate_t, input_t):
    heads, width, _ = rate_t.shape
    rows, total = adj.shape
    col = lambda h: (0, h)
    blk = pl.BlockSpec((rows, width), col)
    row8 = pl.BlockSpec((8, width), col)
    square = pl.BlockSpec((1, width, width), lambda h: (h, 0, 0))
    return pl.pallas_call(
        _mix_bwd_kernel,
        grid=(heads,),
        in_specs=[
            blk, blk, row8, blk, row8, blk,
            pl.BlockSpec((rows + halo, 1), lambda h: (0, 0)),
            pl.BlockSpec((16, width), col),
            square, square,
        ],
        out_specs=[blk, square, square, row8],
        out_shape=[
            jax.ShapeDtypeStruct((rows, total), f32),
            jax.ShapeDtypeStruct((heads, width, width), bf16),
            jax.ShapeDtypeStruct((heads, width, width), bf16),
            jax.ShapeDtypeStruct((8, total), f32),
        ],
        name="mix_bwd", cost_estimate=cost(14),
    )(adj, tail, hand, full, enter, conv, off_ext, vec, rate_t, input_t)


def _conv_bwd_kernel(gc_ref, next_ref, bx_ref, off_ref, vec_ref, gx_ref, sums_ref, ext_ref):
    rows = gc_ref.shape[0]
    vec = vec_ref[...]
    gc = gc_ref[...]
    ext_ref[0:rows] = gc
    ext_ref[rows : rows + halo] = next_ref[...]
    off = off_ref[0:rows]
    gx = gc * vec[0:1]
    sums_ref[0:1] = jnp.sum(gc * bx_ref[halo : halo + rows], axis=0, keepdims=True)
    for lag in range(1, 4):
        gx = gx + jnp.where(off_ref[lag : lag + rows] >= lag, ext_ref[lag : lag + rows], 0.0) * vec[lag : lag + 1]
        term = jnp.where(off >= lag, gc * bx_ref[halo - lag : halo - lag + rows], 0.0)
        sums_ref[lag : lag + 1] = jnp.sum(term, axis=0, keepdims=True)
    sums_ref[4:5] = jnp.sum(gc, axis=0, keepdims=True)
    sums_ref[5:8] = jnp.zeros((3, gc.shape[1]), f32)
    gx_ref[...] = gx.astype(bf16)


def conv_bwd(gc, gc_next, bx_ext, off_ext, vec, width):
    rows, total = gc.shape
    col = lambda h: (0, h)
    return pl.pallas_call(
        _conv_bwd_kernel,
        grid=(total // width,),
        in_specs=[
            pl.BlockSpec((rows, width), col),
            pl.BlockSpec((halo, width), col),
            pl.BlockSpec((rows + halo, width), col),
            pl.BlockSpec((rows + halo, 1), lambda h: (0, 0)),
            pl.BlockSpec((16, width), col),
        ],
        out_specs=[pl.BlockSpec((rows, width), col), pl.BlockSpec((8, width), col)],
        out_shape=[jax.ShapeDtypeStruct((rows, total), bf16), jax.ShapeDtypeStruct((8, total), f32)],
        scratch_shapes=[pltpu.VMEM((rows + halo, width), f32)],
        name="conv_bwd", cost_estimate=cost(7),
    )(gc, gc_next, bx_ext, off_ext, vec)


def after(x, *deps):
    return lax.optimization_barrier((x, deps))[0]


def per_device(
    tokens, cotangent, lengths, seq_deal, mixer_gain, recur_weight, gelu_weight, kernel_taps, kernel_bias,
    decay_param, rate_bias, input_bias, rate_blocks, input_blocks, mixer_out, feed_gain, feed_gate, feed_up,
    feed_down,
):
    groups = lax.axis_size("dp")
    lanes = lax.axis_size("tensor")
    bits = groups.bit_length() - 1
    g = lax.axis_index("dp")
    t = lax.axis_index("tensor")
    lane = t[None].astype(jnp.int32)
    device = g * lanes + t
    rows, width = tokens.shape
    piece_rows = rows // groups
    feats = mixer_gain.shape[0]
    chans = recur_weight.shape[1]
    lru_total = chans * lanes
    head_width = rate_blocks.shape[1]
    wide = tile_of(lru_total, 640)

    def swap(x, bit):
        return lax.ppermute(x, "dp", [(i, i ^ (1 << bit)) for i in range(groups)])

    def up(x):
        return lax.ppermute(x, "tensor", [(i, (i + 1) % lanes) for i in range(lanes)])

    def shift(x, by):
        return lax.ppermute(x, "tensor", [(i, i + by) for i in range(lanes) if 0 <= i + by < lanes])

    def gather_near(part, *deps):
        part = (after(part, *deps) if deps else part)[None]
        for bit in range(3, bits):
            part = jnp.concatenate([part, swap(part, bit)], axis=0)
        return part, swap(part, 1), swap(part, 2)

    def gather_far(near, *deps):
        part, from_x, from_y = near
        half = feats // 2
        low, high = after((from_y[..., :half, :], from_x[..., half:, :]), *deps)
        return part, from_x, from_y, swap(low, 1), swap(high, 2)

    def gather_outer(part, *deps):
        part = (after(part, *deps) if deps else part)[None]
        for bit in range(3, bits):
            part = jnp.concatenate([part, swap(part, bit)], axis=0)
        from_x, from_y = swap(part, 1), swap(part, 2)
        half = feats // 2
        low, high = swap(from_y[..., :half, :], 1), swap(from_x[..., half:, :], 2)
        return part, from_x, from_y, low, high

    def reduce_far(blocks):
        return swap(blocks[3], 1), swap(blocks[4], 2)

    def reduce_near(blocks, far):
        half = feats // 2
        to_x, to_y = blocks[1], blocks[2]
        y_low = to_y[..., :half, :].astype(f32) + far[0].astype(f32)
        to_y = jnp.concatenate([y_low.astype(bf16), to_y[..., half:, :]], axis=-2)
        x_high = to_x[..., half:, :].astype(f32) + far[1].astype(f32)
        to_x = jnp.concatenate([to_x[..., :half, :], x_high.astype(bf16)], axis=-2)
        return swap(to_x, 1), swap(to_y, 2)

    def reduce_end(blocks, near):
        total = blocks[0].astype(f32) + near[0].astype(f32) + near[1].astype(f32)
        for bit in reversed(range(3, bits)):
            keep = total.shape[0] // 2
            total = total[:keep] + swap(total[keep:].astype(bf16), bit).astype(f32)
        return total[0]

    feat_ids = jnp.arange(width, dtype=jnp.int32)
    block_ids, within = feat_ids // feats, feat_ids % feats
    rel_at = 2 * (block_ids % (groups // 2)) + block_ids // (groups // 2)
    from_in = (g ^ rel_at) * feats + within
    rel_of = g ^ block_ids
    from_out = ((rel_of & 1) * (groups // 2) + (rel_of >> 1)) * feats + within

    def vectors_out(x):
        lead = x.shape[0]
        y = jnp.moveaxis(x.reshape((lead,) + (2,) * bits + (feats,)), 1, bits)
        for bit in range(bits):
            y = jnp.where((g >> bit) & 1 == 1, jnp.flip(y, bits - bit), y)
        return y.reshape(lead, width)

    slots = jnp.arange(groups, dtype=jnp.int32)
    places = jnp.arange(seq_deal.shape[0], dtype=jnp.int32)
    own_ids = device * groups + slots
    place_of = jnp.sum(jnp.where(own_ids[:, None] == seq_deal[None, :], places[None, :], 0), axis=1)
    target = place_of // groups // lanes
    source = jnp.sum(jnp.where(own_ids[:, None] == places[None, :], seq_deal[None, :], 0), axis=1) // groups // lanes
    rel_group = slots ^ g
    send_order = jnp.sum(jnp.where(target[None, :] == rel_group[:, None], slots[None, :], 0), axis=1)
    back_order = jnp.sum(jnp.where(source[None, :] == rel_group[:, None], slots[None, :], 0), axis=1)

    def exchange(pieces, order):
        for bit in order:
            view = pieces.reshape((groups >> (bit + 1), 2, (1 << bit) * piece_rows, width))
            got = swap(view[:, 1], bit)
            pieces = jnp.stack([view[:, 0], got], axis=1)
        return pieces.reshape(groups, piece_rows, width)

    def deal(x, order):
        sent = pick_pieces(x.reshape(groups, piece_rows, width), send_order)
        return turn_feats(pick_pieces(exchange(sent, order), source ^ g).reshape(rows, width), from_in)

    def undeal(x, order):
        sent = pick_pieces(turn_feats(x, from_out).reshape(groups, piece_rows, width), back_order)
        return pick_pieces(exchange(sent, order), target ^ g).reshape(rows, width)

    x_first = [1, 2] + list(range(3, bits)) + [0]
    y_first = [2, 1] + list(range(3, bits)) + [0]

    row_place = t * rows + jnp.arange(rows + halo, dtype=jnp.int32)
    begins = jnp.zeros_like(row_place)
    start = jnp.int32(0)
    for s in range(lengths.shape[1]):
        begins = jnp.where(row_place >= start, start, begins)
        start = start + lengths[0, s]
    off_ext = jnp.where(row_place < lanes * rows, row_place - begins, -1)[:, None]

    chan_count = kernel_bias.shape[0]
    small = jnp.concatenate(
        [kernel_taps.reshape(-1), kernel_bias, rate_bias, input_bias, decay_param, mixer_gain, feed_gain]
    )
    small = jnp.pad(small, (0, -small.shape[0] % 128))[None, None]
    step = 1
    while step < lanes:
        got = lax.ppermute(small, "tensor", [(i, i ^ step) for i in range(lanes)])
        small = jnp.concatenate([small, got], axis=0)
        step *= 2
    small = small.reshape(1, lanes, -1)
    for bit in range(bits):
        small = jnp.concatenate([small, swap(small, bit)], axis=0)

    x_low = deal(tokens, x_first)
    x = x_low.astype(f32)
    cot_low = deal(cotangent, y_first)

    def over_lanes(w):
        return lax.all_gather(w, "tensor", axis=0)

    lanes_x = over_lanes(recur_weight)
    lanes_y = over_lanes(gelu_weight)
    blocks = jnp.stack([jnp.swapaxes(rate_blocks, 1, 2), jnp.swapaxes(input_blocks, 1, 2)])
    blocks = lax.all_gather(after(blocks, lanes_x), "dp", axis=2, tiled=True)
    rate_t, input_t = blocks[0], blocks[1]
    lanes_o = over_lanes(flip_weight(mixer_out))
    cot_all = lax.all_gather(after(cot_low, lanes_o), "tensor", axis=0, tiled=True)

    def with_other(own):
        return own, swap(own, 0)

    part_g = gather_outer(feed_gate)
    part_x = gather_outer(lanes_x)
    part_y = gather_outer(lanes_y, part_g[3:])
    wx = with_other(join_lanes(*part_x))
    part_o = gather_outer(lanes_o, part_x[3:], cot_low)
    wg = with_other(join_feats(*part_g))
    wy = with_other(join_lanes(*part_y))
    wo = with_other(join_lanes(*part_o))

    chan_ids = jnp.arange(lru_total, dtype=jnp.int32)
    chan_lane, chan_dp, chan_in = chan_ids // chans, chan_ids % chans // chan_count, chan_ids % chan_count
    from_chan = ((chan_dp ^ g) * lanes + (chan_lane ^ t)) * chan_count + chan_in
    from_gain = (g ^ rel_at ^ g) * feats + within
    small_cols = 8 * chan_count
    chan_part = small[:, :, :small_cols].reshape(groups, lanes, 8, chan_count)
    chan_part = jnp.moveaxis(chan_part, 2, 0).reshape(8, lru_total)
    gain_part = small[:, 0, small_cols : small_cols + 2 * feats].reshape(groups, 2, feats)
    gain_part = jnp.swapaxes(gain_part, 0, 1).reshape(2, width)
    chan_vec = turn_feats(jnp.pad(chan_part, ((0, 8), (0, 0))), from_chan).astype(f32)
    gains = turn_feats(jnp.pad(gain_part, ((0, 14), (0, 0))), from_gain).astype(f32)
    gain_first, gain_second = gains[0], gains[1]
    vec = jnp.concatenate(
        [
            chan_vec[:7],
            jax.nn.softplus(-chan_vec[7:8]),
            jax.nn.sigmoid(-chan_vec[7:8]),
            jnp.zeros((7, lru_total), f32),
        ],
        axis=0,
    )

    normed_low = (x * inv_rms(x) * gain_first[None]).astype(bf16)
    normed_ext = jnp.concatenate([up(normed_low[rows - halo :]), normed_low], axis=0)
    bx_ext = rows_into(normed_ext, wx)
    near_u = gather_near(feed_up, part_y[3:], bx_ext)
    by = rows_into(normed_low, wy)
    conv_low, state_loc, prod_loc = mix_fwd(bx_ext, off_ext, vec, rate_t, input_t)
    near_d = gather_near(flip_weight(feed_down), part_o[3:], state_loc)
    edge = jnp.concatenate([state_loc[rows - 1 :], prod_loc[rows - 1 :], jnp.zeros((6, lru_total), f32)], axis=0)

    def carry_in(edge, direction):
        total = jnp.zeros((1, lru_total), f32)
        factor = jnp.ones((1, lru_total), f32)
        for by_lanes in range(1, lanes):
            far = shift(edge, direction * by_lanes)
            total = total + factor * far[0:1]
            factor = factor * far[1:2]
        return jnp.broadcast_to(total, (8, lru_total))

    enter = carry_in(edge, 1)
    state, mixed = mix_out(state_loc, prod_loc, enter, by, wide)
    middle = x + rows_back([(mixed, wo)])
    ns_low = (middle * inv_rms(middle) * gain_second[None]).astype(bf16)
    part_u = gather_far(near_u, ns_low)
    part_d = gather_far(near_d, ns_low)
    ns_rows = [ns_low]
    for _ in range(lanes - 1):
        ns_rows.append(up(ns_rows[-1]))

    part_u = (after(part_u[0], ns_rows[1]),) + tuple(part_u[1:])
    part_d = (after(part_d[0], ns_rows[1]),) + tuple(part_d[1:])
    wu = with_other(join_feats(*part_u))
    wd = with_other(join_feats(*part_d))

    pair = 2
    hidden, g_gate, g_up = [], [], []
    total = None
    for at in range(0, lanes, pair):
        first = ns_rows[at] if total is None else after(ns_rows[at], total)
        h, gg, gu = feed_pair([first] + ns_rows[at + 1 : at + pair], cot_all, at, wg, wu, wd, lane, lanes)
        hidden.append(h)
        g_gate.append(gg)
        g_up.append(gu)
        if total is None:
            total = feed_back([(gg, wg), (gu, wu)], 1, rows, [], bf16)

    def other_half(lefts, rights, *deps, **kind):
        first = after(rights[0], *deps) if deps else rights[0]
        return weight_grad(lefts, [first] + rights[1:], 1, feats, lane, lanes, **kind)

    def own_half(lefts, rights, other, *deps, **kind):
        first = after(rights[0], *deps) if deps else rights[0]
        return weight_grad(lefts, [first] + rights[1:], 0, feats, lane, lanes, got=swap(other, 0), **kind)

    def second_part(k, total, *deps):
        terms = [(after(g_gate[k // pair], *deps) if deps else g_gate[k // pair], wg), (g_up[k // pair], wu)]
        return feed_back(terms, k % pair, rows, [] if total is None else [up(total)], f32 if k == 0 else bf16)

    cot_parts = [(cot_all, rows, k) for k in range(lanes)]
    for k in range(2, lanes - 2):
        total = second_part(k, total)
    total = second_part(lanes - 2, total)
    other_down = other_half(cot_parts, hidden, total)
    other_gate = other_half(ns_rows, g_gate, other_down)
    own_down = own_half(cot_parts, hidden, other_down, other_gate)
    far_down = reduce_far(own_down)
    own_gate = own_half(ns_rows, g_gate, other_gate, own_down)
    far_gate = reduce_far(own_gate)
    total = second_part(lanes - 1, total, own_gate, far_down)
    near_down = reduce_near(own_down, far_down)
    other_up = other_half(ns_rows, g_up, total)
    near_gate = reduce_near(own_gate, far_gate)
    own_up = own_half(ns_rows, g_up, other_up, far_gate)
    far_up = reduce_far([after(b, near_down) for b in own_up])
    g_second = second_part(0, total, own_up, near_down)
    near_up = reduce_near(own_up, far_up)

    g_mid_part, d_gain_second = norm_back(middle, gain_second[None], g_second)
    g_middle = cot_low.astype(f32) + g_mid_part
    g1 = g_middle.astype(bf16)

    def lane_sum(blocks):
        return lax.psum_scatter(blocks.astype(bf16), "tensor", scatter_dimension=0).astype(f32)

    by_lane = dict(by_lane=True)
    other_out = other_half([g1], [mixed], **by_lane)
    gm = rows_into(after(g1, other_out, near_gate), wo)
    own_out = own_half([g1], [mixed], other_out, gm, far_up, **by_lane)
    far_out = reduce_far(own_out)
    gy_low, adj_loc, tail, edge_back = mix_adj(after(gm, own_out), by, state, conv_low, off_ext, vec, rate_t)
    hand_got = shift(edge_back, -1)
    span = 1
    while span < lanes - 1:
        hand_far = shift(hand_got, -span)
        rows01 = [hand_got[0:1] + hand_got[1:2] * hand_far[0:1], hand_got[1:2] * hand_far[1:2]]
        hand_got = jnp.concatenate(rows01 + [jnp.zeros((6, lru_total), f32)], axis=0)
        span *= 2
    hand = jnp.broadcast_to(hand_got[0:1], (8, lru_total))
    other_y = other_half([normed_low], [gy_low], near_up, **by_lane)
    near_out = reduce_near(own_out, far_out)
    feed_sum = feed_out([after(hidden[0], other_y, far_out)] + hidden[1:], wd, lane, lanes)
    feed_sum = lax.psum_scatter(feed_sum, "tensor", scatter_dimension=0, tiled=True)
    own_y = own_half([normed_low], [gy_low], other_y, **by_lane)
    far_y = reduce_far(own_y)
    g_conv, d_rate, d_input, sums_gate = mix_bwd(
        after(adj_loc, own_y), tail, hand, state, enter, conv_low, off_ext, vec, rate_t, input_t
    )
    gc_next = lax.ppermute(g_conv[:halo], "tensor", [(i, (i - 1) % lanes) for i in range(lanes)])
    gx_low, sums_conv = conv_bwd(g_conv, gc_next, bx_ext, off_ext, vec, wide)
    near_y = reduce_near(own_y, far_y)
    other_x = other_half([normed_low], [gx_low], near_out, **by_lane)
    g_first = rows_back([(after(gx_low, other_x), wx), (gy_low, wy)])
    own_x = own_half([normed_low], [gx_low], other_x, far_y, **by_lane)
    far_x = reduce_far(own_x)
    d_down = reduce_end(own_down, near_down)
    d_gate = reduce_end(own_gate, near_gate)
    d_up = reduce_end(own_up, near_up)
    d_out = lane_sum(reduce_end(own_out, near_out))
    near_x = reduce_near(own_x, far_x)
    d_y = lane_sum(reduce_end(own_y, near_y))
    d_x = lane_sum(reduce_end(own_x, near_x))
    g_tok_part, d_gain_first = norm_back(x, gain_first[None], g_first)
    tokens_grad = undeal((g_middle + g_tok_part).astype(bf16), y_first)
    block_out = undeal((middle + feed_sum.astype(f32)).astype(bf16), x_first)

    d_blocks = lax.psum_scatter(jnp.stack([d_rate, d_input]), "dp", scatter_dimension=2, tiled=True)
    d_blocks = jnp.swapaxes(lax.psum(d_blocks, "tensor"), 2, 3).astype(f32)
    d_gains = vectors_out(jnp.stack([d_gain_first, d_gain_second]))
    vectors = jnp.concatenate([sums_conv[:5], sums_gate[:3], d_gains, jnp.zeros((6, width), f32)], axis=0)
    for bit in range(bits):
        vectors = vectors + swap(vectors, bit)
    step = 1
    while step < lanes:
        vectors = vectors + lax.ppermute(vectors, "tensor", [(i, i ^ step) for i in range(lanes)])
        step *= 2
    chan_grad = lax.dynamic_slice_in_dim(vectors[:8], (t * groups + g) * chan_count, chan_count, axis=1)
    gain_grad = lax.dynamic_slice_in_dim(vectors[8:10], g * feats, feats, axis=1)

    return (
        block_out,
        tokens_grad,
        gain_grad[0],
        d_x,
        d_y,
        chan_grad[0:4],
        chan_grad[4],
        chan_grad[5],
        chan_grad[6],
        chan_grad[7],
        d_blocks[0],
        d_blocks[1],
        d_out.T,
        gain_grad[1],
        d_gate,
        d_up,
        d_down.T,
    )


def solution(mesh):
    rows = P(("dp", "tensor"), None)
    feat = P("dp")
    chan = P(("tensor", "dp"))
    taps = P(None, ("tensor", "dp"))
    into = P("dp", "tensor")
    back = P("tensor", "dp")
    blocks = P(None, None, "dp")
    in_specs = (
        rows, rows, P("dp", None), P(), feat, into, into, taps, chan, chan, chan, chan, blocks, blocks, back, feat,
        into, into, back,
    )
    out_specs = (
        rows, rows, feat, into, into, taps, chan, chan, chan, chan, blocks, blocks, back, feat, into, into, back,
    )
    return jax.shard_map(per_device, mesh=mesh, in_specs=in_specs, out_specs=out_specs, check_vma=False)
```
